32 devices in a mesh: dp: 8 (over y, x, core), tensor: 4 (over z).
Axes of the slice: x: 2, y: 2, z: 4, core: 2. Of those that a mesh axis runs over, the one named last changes fastest.
Arguments:
- block_input: bfloat16 [4096, 1024], P(('dp', 'tensor')), may hold values from -6 to 6
- output_cotangent: bfloat16 [4096, 1024], P(('dp', 'tensor')), may hold values from -6 to 6
- first_gain: bfloat16 [1024], replicated, may hold values from 0.5 to 1.5
- first_shift: bfloat16 [1024], replicated, may hold values from -4 to 4
- project_in: bfloat16 [1024, 3, 1024], P('dp', None, 'tensor'), may hold values from -0.1875 to 0.1875
- query_value_bias: bfloat16 [2, 1024], P(None, 'tensor'), may hold values from -4 to 4
- project_out: bfloat16 [1024, 1024], P('tensor', 'dp'), may hold values from -0.5 to 0.5
- project_out_bias: bfloat16 [1024], replicated, may hold values from -4 to 4
- second_gain: bfloat16 [1024], replicated, may hold values from 0.5 to 1.5
- second_shift: bfloat16 [1024], replicated, may hold values from -4 to 4
- expand_weight: bfloat16 [1024, 4096], P('dp', 'tensor'), may hold values from -0.1875 to 0.1875
- expand_bias: bfloat16 [4096], P('tensor'), may hold values from -4 to 4
- shrink_weight: bfloat16 [4096, 1024], P('tensor', 'dp'), may hold values from -0.125 to 0.125
- shrink_bias: bfloat16 [1024], replicated, may hold values from -4 to 4
Outputs:
- block_output: bfloat16 [4096, 1024], P(('dp', 'tensor'))
- input_grad: bfloat16 [4096, 1024], P(('dp', 'tensor'))
- first_gain_grad: float32 [1024], replicated
- first_shift_grad: float32 [1024], replicated
- project_in_grad: float32 [1024, 3, 1024], P('dp', None, 'tensor')
- query_value_bias_grad: float32 [2, 1024], P(None, 'tensor')
- project_out_grad: float32 [1024, 1024], P('tensor', 'dp')
- project_out_bias_grad: float32 [1024], replicated
- second_gain_grad: float32 [1024], replicated
- second_shift_grad: float32 [1024], replicated
- expand_weight_grad: float32 [1024, 4096], P('dp', 'tensor')
- expand_bias_grad: float32 [4096], P('tensor')
- shrink_weight_grad: float32 [4096, 1024], P('tensor', 'dp')
- shrink_bias_grad: float32 [1024], replicated
The draws below stay inside these ranges and needn't reach their ends.
All inputs are finite; a program needn't handle non-finite values.
Results may differ from the reference program's by a relative error of at most 0.019.
Values may be sent and summed in bfloat16 or wider, within the bound.
No kernel may reach another device: no remote copies, remote signals or barrier semaphores. Data moves between devices by JAX's collectives and lax.ppermute only.
A program may use at most 64 MiB of HBM per device.

```python
import math
import jax
import jax.numpy as jnp
from jax import lax

D = 1024
HEADS = 16
HEAD = 64
FF = 4096
SEQ = 512
TOKENS = 4096
N_DP = 8


def level_of(own_key, shape, shards, smallest, top_value):
    level, own = 1.0, jax.random.fold_in(own_key, 6)
    for dim, blocks in shards:
        steps = jnp.exp(jax.random.uniform(jax.random.fold_in(own, dim), (blocks,), jnp.float32, smallest / len(shards), top_value / len(shards)))
        level = level * jnp.repeat(steps, shape[dim] // blocks).reshape([-1 if axis == dim else 1 for axis in range(len(shape))])
    return level


def noise(key, dims, width, reach, pieces=(), held_as=jnp.bfloat16):
    drawn = jax.random.normal(key, dims, jnp.float32) * width
    if len(pieces) > 0:
        drawn = level_of(key, dims, pieces, -0.22, 0.18) * drawn
    return jnp.clip(drawn, min=-reach, max=reach).astype(held_as)


def setup_inputs(seed: int = 0) -> dict:
    seeds = jax.random.split(jax.random.key(seed), 15)
    return {
        "block_input": noise(seeds[0], (TOKENS, D), 1.0, 6.0, ((0, 32),)),
        "output_cotangent": noise(seeds[1], (TOKENS, D), 1.0, 6.0, ((0, 32),)),
        "first_gain": jnp.clip(1.0 + 0.1 * jax.random.normal(seeds[2], (D,), jnp.float32), 0.5, 1.5).astype(jnp.bfloat16),
        "first_shift": noise(seeds[3], (D,), 0.3, 4.0),
        "project_in": noise(seeds[4], (D, 3, D), D ** -0.5, 0.1875, ((0, 8), (2, 4))),
        "query_value_bias": noise(seeds[5], (2, D), 0.3, 4.0, ((1, 4),)),
        "project_out": noise(seeds[6], (D, D), (D // 8) ** -0.5, 0.5, ((0, 4), (1, 8))),
        "project_out_bias": noise(seeds[7], (D,), 0.3, 4.0),
        "second_gain": jnp.clip(1.0 + 0.1 * jax.random.normal(seeds[8], (D,), jnp.float32), 0.5, 1.5).astype(jnp.bfloat16),
        "second_shift": noise(seeds[9], (D,), 0.3, 4.0),
        "expand_weight": noise(seeds[10], (D, FF), D ** -0.5, 0.1875, ((0, 8), (1, 4))),
        "expand_bias": noise(seeds[11], (FF,), 0.5, 4.0, ((0, 4),)),
        "shrink_weight": noise(seeds[12], (FF, D), (FF // 2) ** -0.5, 0.125, ((0, 4), (1, 8))),
        "shrink_bias": noise(seeds[13], (D,), 0.3, 4.0),
    }


@jax.custom_vjp
def low(v):
    return lax.optimization_barrier(v.astype(jnp.bfloat16)).astype(jnp.float32)

@jax.custom_vjp
def low_back(v):
    return v

def low_keep(v):
    return (low(v), None)

def low_pass(kept, grad):
    return (grad,)

def back_keep(v):
    return (v, None)

def back_low(kept, grad):
    return (low(grad),)
low.defvjp(low_keep, low_pass)
low_back.defvjp(back_keep, back_low)
HIGH = lax.Precision.HIGHEST

def layer_norm(values, norm_gain, norm_shift):
    average = lax.optimization_barrier(jnp.mean(values, axis=-1, keepdims=True))
    centered = values - average
    variance = lax.optimization_barrier(jnp.mean(centered * centered, axis=-1, keepdims=True))
    return centered * lax.rsqrt(variance + 1e-05) * norm_gain + norm_shift

def attend_one(triple):
    queries, keys_all, values_all = triple
    product = jnp.einsum('qhd,khd->hqk', queries, keys_all, precision=HIGH)
    position = jnp.arange(SEQ)
    distance = (position[:, None] - position[None, :]).astype(jnp.float32)
    head_ids = (jnp.arange(HEADS) + 1).astype(jnp.float32)
    slopes = jnp.exp2(-8.0 * head_ids / HEADS)
    scores = product * HEAD ** (-0.5) - slopes[:, None, None] * distance[None]
    scores = low_back(scores)
    scores = jnp.where(distance[None] >= 0, scores, -1e+30)
    soft_weights = low(jax.nn.softmax(scores, axis=-1))
    return jnp.einsum('hqk,khd->qhd', soft_weights, values_all, precision=HIGH)

def forward(block_in, first_gain, first_shift, project_in, query_value_bias, project_out, project_out_bias, second_gain, second_shift, expand_weight, expand_bias, shrink_weight, shrink_bias):
    batch = block_in.shape[0]
    normed_one = low(layer_norm(block_in, first_gain, first_shift))
    mixed = jnp.einsum('bsd,dcf->bscf', normed_one, project_in, precision=HIGH)
    bias_full = jnp.stack([query_value_bias[0], jnp.zeros_like(query_value_bias[0]), query_value_bias[1]])
    mixed = low(low_back(mixed + bias_full))
    shaped = mixed.reshape(batch, SEQ, 3, HEADS, HEAD)
    context = lax.map(jax.checkpoint(attend_one), (shaped[:, :, 0], shaped[:, :, 1], shaped[:, :, 2]))
    context = low(low_back(context.reshape(batch, SEQ, D)))
    branch = low_back(jnp.einsum('bsf,fd->bsd', context, project_out, precision=HIGH)) + project_out_bias
    middle = block_in + branch
    normed_two = low(layer_norm(middle, second_gain, second_shift))
    hidden = low_back(jnp.einsum('bsd,df->bsf', normed_two, expand_weight, precision=HIGH) + expand_bias)
    active = low(jax.nn.gelu(hidden, approximate=True))
    shrunk = low_back(jnp.einsum('bsf,fd->bsd', active, shrink_weight, precision=HIGH))
    return middle + shrunk + shrink_bias

def reference(block_input, output_cotangent, first_gain, first_shift, project_in, query_value_bias, project_out, project_out_bias, second_gain, second_shift, expand_weight, expand_bias, shrink_weight, shrink_bias):
    params = tuple((item.astype(jnp.float32) for item in (first_gain, first_shift, project_in, query_value_bias, project_out, project_out_bias, second_gain, second_shift, expand_weight, expand_bias, shrink_weight, shrink_bias)))
    groups = math.gcd(N_DP, max(1, 4096 // SEQ))
    rounds = N_DP // groups
    inputs = block_input.astype(jnp.float32).reshape(rounds, groups, SEQ, D)
    upstream = output_cotangent.astype(jnp.float32).reshape(rounds, groups, SEQ, D)

    def one_round(totals, pair):
        block_rows, grad_rows = pair
        result, pullback = jax.vjp(forward, block_rows, *params)
        cotangents = pullback(grad_rows)
        totals = jax.tree.map(jnp.add, totals, tuple(cotangents[1:]))
        return (totals, (result.astype(jnp.bfloat16), cotangents[0].astype(jnp.bfloat16)))
    zeros = tuple((jnp.zeros_like(item) for item in params))
    totals, (outputs, in_grads) = lax.scan(one_round, zeros, (inputs, upstream))
    return (outputs.reshape(TOKENS, D), in_grads.reshape(TOKENS, D), totals[0], totals[1], totals[2], totals[3], totals[4], totals[5], totals[6], totals[7], totals[8], totals[9], totals[10], totals[11])
```

```python
import jax
import jax.numpy as jnp
from jax import lax
from jax.sharding import PartitionSpec as P

HEADS = 16
HEAD = 64
AXES = ("dp", "tensor")
LOW = jnp.bfloat16
WIDE = jnp.float32


def together(*values):
    return lax.optimization_barrier(values)


def stats(rows):
    average = jnp.mean(rows, axis=-1, keepdims=True)
    centered = rows - average
    variance = jnp.mean(centered * centered, axis=-1, keepdims=True)
    scale = lax.rsqrt(variance + 1e-05)
    return centered * scale, scale


def norm_back(grad, gain, unit, scale):
    inner = grad * gain
    first = jnp.mean(inner, axis=-1, keepdims=True)
    second = jnp.mean(inner * unit, axis=-1, keepdims=True)
    return scale * (inner - first - unit * second)


def gelu_local(hidden):
    return jax.nn.gelu(hidden, approximate=True)


def make_body(n_dp, n_t):
    bits = [1 << k for k in range(1, n_dp.bit_length() - 1)]

    def send(value, target):
        pairs = []
        for d in range(n_dp):
            for t in range(n_t):
                goal = target(d, t)
                if goal is not None:
                    pairs.append((d * n_t + t, goal[0] * n_t + goal[1]))
        return lax.ppermute(value, AXES, pairs)

    def swap_z(value, mask):
        return send(value, lambda d, t: (d, t ^ mask))

    def swap_dp(value, mask):
        return send(value, lambda d, t: (d ^ mask, t))

    def bit_of(mask):
        return (lax.axis_index("dp") & mask) != 0

    def spread(value, order):
        out = value.reshape((1,) * len(bits) + value.shape)

        def step(out, mask):
            axis = len(bits) - 1 - bits.index(mask)
            other = swap_dp(out, mask)
            flag = bit_of(mask)
            return jnp.concatenate(
                [jnp.where(flag, other, out), jnp.where(flag, out, other)], axis=axis
            )

        return out, step

    def spread_two(first, second):
        forth, back = bits[::-1], bits
        a, step = spread(first, forth)
        b, _ = spread(second, back)
        for mask_a, mask_b in zip(forth, back):
            a, b = step(a, mask_a), step(b, mask_b)
            a, b = together(a, b)
        return (
            a.reshape((-1,) + first.shape[1:]),
            b.reshape((-1,) + second.shape[1:]),
        )

    def fold_two(first, second):
        forth, back = bits, bits[::-1]
        lead = (2,) * len(bits)
        a = first.reshape(lead + first.shape[1:])
        b = second.reshape(lead + second.shape[1:])

        def step(value, mask):
            axis = len(bits) - 1 - bits.index(mask)
            place = (lax.axis_index("dp") // mask) % 2
            keep = lax.dynamic_slice_in_dim(value, place, 1, axis)
            give = lax.dynamic_slice_in_dim(value, 1 - place, 1, axis)
            other = swap_dp(give.astype(LOW), mask)
            return keep.astype(WIDE) + other.astype(WIDE)

        for mask_a, mask_b in zip(forth, back):
            a, b = step(a, mask_a).astype(LOW), step(b, mask_b).astype(LOW)
            a, b = together(a, b)
        return a.reshape(first.shape[1:]), b.reshape(second.shape[1:])

    def gather_z(value):
        return jnp.concatenate([value] + [swap_z(value, k) for k in range(1, n_t)], axis=0)

    def fold_z(parts):
        total = parts[0].astype(WIDE)
        for k in range(1, n_t):
            total = total + swap_z(parts[k].astype(LOW), k).astype(WIDE)
        return total

    def gather_four(value):
        near = swap_z(value, 1)
        across = swap_dp(value, 1)
        both = swap_dp(near, 1)
        return jnp.concatenate([value, near, across, both], axis=0)

    def fold_four(parts):
        other = swap_dp(parts[2:].astype(LOW), 1)
        half = parts[:2].astype(WIDE) + other.astype(WIDE)
        return half[0] + swap_z(half[1].astype(LOW), 1).astype(WIDE)

    def body(
        block_input,
        output_cotangent,
        first_gain,
        first_shift,
        project_in,
        query_value_bias,
        project_out,
        project_out_bias,
        second_gain,
        second_shift,
        expand_weight,
        expand_bias,
        shrink_weight,
        shrink_bias,
    ):
        rows, width = block_input.shape
        local = project_out.shape[0]
        wide = expand_weight.shape[1]
        heads = local // HEAD
        core = lax.axis_index("dp") % 2
        place = lax.axis_index("tensor")
        gain_one, shift_one = first_gain.astype(WIDE), first_shift.astype(WIDE)
        gain_two, shift_two = second_gain.astype(WIDE), second_shift.astype(WIDE)
        bias_qv = query_value_bias.astype(WIDE)

        part_in = project_in.reshape(project_in.shape[0], 3 * local)
        part_a = part_in[:, : 2 * local]
        part_b = jnp.concatenate([part_in[:, 2 * local :], project_out.T], axis=1)
        rows_all = gather_z(block_input)
        full_a, full_b = spread_two(part_a[None], part_b[None])
        pair = jnp.concatenate([full_a, full_b], axis=-1)
        mate = swap_dp(pair, 1)
        full = jnp.stack([jnp.where(core == 0, pair, mate), jnp.where(core == 0, mate, pair)], 1)
        full = full.reshape(width, 4 * local)
        full_in, full_out = full[:, : 3 * local], full[:, 3 * local :]

        near = jnp.concatenate([expand_weight, shrink_weight.T], axis=1)
        one = send(near, lambda d, t: (d ^ 1, t) if d % 2 else (d ^ 1, t ^ 2))
        two = send(near, lambda d, t: (d, t ^ 2) if d % 2 else None)
        both = jnp.stack([jnp.where(core == 0, near, one), jnp.where(core == 0, one, two)])
        bias_far = send(expand_bias, lambda d, t: (d, t ^ 2))
        bias_expand = jnp.where(core == 0, expand_bias, bias_far).astype(WIDE)

        wide_rows = rows_all.astype(WIDE)
        unit_all, scale_all = stats(wide_rows)
        normed_all = (unit_all * gain_one + shift_one).astype(LOW)
        tokens = normed_all.shape[0]
        mixed = jnp.dot(normed_all, full_in, preferred_element_type=WIDE)
        bias_full = jnp.concatenate([bias_qv[0], jnp.zeros_like(bias_qv[0]), bias_qv[1]])
        mixed = (mixed + bias_full).astype(LOW)
        shaped = mixed.reshape(tokens, 3, heads, HEAD)
        queries, keys, values = shaped[:, 0], shaped[:, 1], shaped[:, 2]
        chunk = jnp.arange(tokens) // rows
        position = (chunk ^ place) * rows + jnp.arange(tokens) % rows
        distance = (position[:, None] - position[None, :]).astype(WIDE)
        head_ids = (place * heads + jnp.arange(heads) + 1).astype(WIDE)
        slopes = jnp.exp2(-8.0 * head_ids / HEADS)

        def scores_of(queries, keys):
            product = jnp.einsum("qhd,khd->hqk", queries, keys, preferred_element_type=WIDE)
            scores = product * HEAD ** (-0.5) - slopes[:, None, None] * distance[None]
            return jnp.where(distance[None] >= 0, scores, -1e30)

        scores = scores_of(queries, keys)
        top = jnp.max(scores, axis=-1, keepdims=True)
        log_total = top + jnp.log(jnp.sum(jnp.exp(scores - top), axis=-1, keepdims=True))
        soft_low = jnp.exp(scores - log_total).astype(LOW)
        context = jnp.einsum("hqk,khd->qhd", soft_low, values, preferred_element_type=WIDE)
        context = context.reshape(tokens, local).astype(LOW)
        branch = jnp.einsum("sf,df->sd", context, full_out, preferred_element_type=WIDE)
        branch = branch.reshape(n_t, rows, width)
        top_low = output_cotangent
        tops = gather_four(top_low)
        expand_pair, shrink_pair = both[:, :, :wide], both[:, :, wide:]
        full_expand, full_shrink = spread_two(
            expand_pair.reshape(-1, wide)[None], shrink_pair.reshape(-1, wide)[None]
        )
        full_expand = full_expand.reshape(width, wide)
        full_shrink = full_shrink.reshape(width, wide)
        middle = block_input.astype(WIDE) + fold_z(branch) + project_out_bias.astype(WIDE)

        unit_two, scale_two = stats(middle)
        second_all = gather_four((unit_two * gain_two + shift_two).astype(LOW))
        hidden = jnp.dot(second_all, full_expand, preferred_element_type=WIDE) + bias_expand
        active, gelu_pull = jax.vjp(gelu_local, hidden)
        active = active.astype(LOW)
        active_grad = jnp.dot(tops, full_shrink, preferred_element_type=WIDE)
        (hidden_grad,) = gelu_pull(active_grad)
        hidden_grad = hidden_grad.astype(LOW)
        second_part = jnp.einsum("sf,df->sd", hidden_grad, full_expand, preferred_element_type=WIDE)
        second_grad = fold_four(second_part.reshape(4, rows, width))
        shrunk = jnp.einsum("sf,df->sd", active, full_shrink, preferred_element_type=WIDE)
        shrunk = fold_four(shrunk.reshape(4, rows, width))
        result = middle + shrunk + shrink_bias.astype(WIDE)
        expand_bias_part = jnp.sum(hidden_grad.astype(WIDE), axis=0)
        expand_grad = jnp.einsum("sd,sf->df", second_all, hidden_grad, preferred_element_type=WIDE)
        shrink_grad = jnp.einsum("sd,sf->df", tops, active, preferred_element_type=WIDE)
        blocks = n_dp // 2
        expand_sum, shrink_sum = fold_two(
            expand_grad.astype(LOW).reshape(blocks, -1, wide),
            shrink_grad.astype(LOW).reshape(blocks, -1, wide),
        )
        share = jnp.concatenate([expand_sum, shrink_sum], axis=1).reshape(2, -1, 2 * wide)
        away = send(
            jnp.where(core == 0, share[1], share[0]),
            lambda d, t: (d ^ 1, t ^ 2) if d % 2 else (d ^ 1, t),
        )
        far = send(share[1], lambda d, t: (d, t ^ 2) if d % 2 else None)
        feed_sum = away.astype(WIDE) + jnp.where(core == 0, share[0], far).astype(WIDE)

        upstream = output_cotangent.astype(WIDE)
        middle_grad = upstream + norm_back(second_grad, gain_two, unit_two, scale_two)
        middle_all = gather_z(middle_grad.astype(LOW))

        out_grad = jnp.einsum("sd,sf->df", middle_all, context, preferred_element_type=WIDE)
        context_grad = jnp.dot(middle_all, full_out, preferred_element_type=WIDE)
        context_grad = context_grad.astype(LOW).reshape(tokens, heads, HEAD)
        soft = jnp.exp(scores_of(queries, keys) - log_total)
        value_grad = jnp.einsum(
            "hqk,qhd->khd", soft.astype(LOW), context_grad, preferred_element_type=WIDE
        )
        soft_grad = jnp.einsum("qhd,khd->hqk", context_grad, values, preferred_element_type=WIDE)
        score_grad = soft * (soft_grad - jnp.sum(soft * soft_grad, axis=-1, keepdims=True))
        score_grad = score_grad.astype(LOW)
        query_grad = jnp.einsum("hqk,khd->qhd", score_grad, keys, preferred_element_type=WIDE)
        key_grad = jnp.einsum("hqk,qhd->khd", score_grad, queries, preferred_element_type=WIDE)
        mixed_grad = jnp.stack(
            [query_grad * HEAD ** (-0.5), key_grad * HEAD ** (-0.5), value_grad], axis=1
        )
        mixed_grad = mixed_grad.reshape(tokens, 3 * local).astype(LOW)
        mixed_sums = jnp.sum(mixed_grad.astype(WIDE), axis=0)
        first_part = jnp.einsum("sf,df->sd", mixed_grad, full_in, preferred_element_type=WIDE)
        first_grad = fold_z(first_part.reshape(n_t, rows, width))
        gain_one_part = jnp.sum(first_part * unit_all, axis=0)
        shift_one_part = jnp.sum(first_part, axis=0)
        in_grad = jnp.einsum("sd,sf->df", normed_all, mixed_grad, preferred_element_type=WIDE)

        grads = jnp.concatenate([in_grad, out_grad], axis=1).astype(LOW)
        grads = grads.reshape(blocks, 2, -1, 4 * local)
        mine = lax.dynamic_slice_in_dim(grads, core, 1, 1)
        other = lax.dynamic_slice_in_dim(grads, 1 - core, 1, 1)
        grads = (mine.astype(WIDE) + swap_dp(other, 1).astype(WIDE)).astype(LOW)
        grads = grads.reshape(blocks, -1, 4 * local)
        sum_a, sum_b = fold_two(grads[:, :, : 2 * local], grads[:, :, 2 * local :])
        in_sum = jnp.concatenate([sum_a, sum_b[:, :local]], axis=1).astype(WIDE)
        out_sum = sum_b[:, local:].astype(WIDE).T

        unit = unit_all[:rows]
        scale = scale_all[:rows]
        input_grad = middle_grad + norm_back(first_grad, gain_one, unit, scale)
        slot = jnp.arange(n_t)[:, None]
        bias_slots = jnp.where(slot == (place ^ (2 * core)), expand_bias_part[None], 0.0)
        qv_parts = jnp.stack([mixed_sums[:local], mixed_sums[2 * local :]])
        qv_slots = jnp.where(slot[None] == place, qv_parts[:, None], 0.0)
        vectors = jnp.concatenate(
            [
                jnp.stack(
                    [
                        gain_one_part,
                        shift_one_part,
                        jnp.sum(middle_grad, axis=0),
                        jnp.sum(second_grad * unit_two, axis=0),
                        jnp.sum(second_grad, axis=0),
                        jnp.sum(upstream, axis=0),
                    ]
                ),
                bias_slots.reshape(-1, width),
                qv_slots.reshape(2, -1),
            ],
            axis=0,
        )
        for mask in [1] + bits:
            vectors = vectors + swap_dp(vectors, mask)
        for mask in (1, 2):
            vectors = vectors + swap_z(vectors, mask)
        bias_slots = vectors[6:-2].reshape(n_t, wide)
        expand_bias_sum = lax.dynamic_index_in_dim(bias_slots, place, 0, keepdims=False)
        qv_slots = vectors[-2:].reshape(2, n_t, local)
        qv_sum = lax.dynamic_index_in_dim(qv_slots, place, 1, keepdims=False)
        return (
            result.astype(LOW),
            input_grad.astype(LOW),
            vectors[0],
            vectors[1],
            in_sum.reshape(project_in.shape),
            qv_sum,
            out_sum,
            vectors[2],
            vectors[3],
            vectors[4],
            feed_sum[:, :wide],
            expand_bias_sum,
            feed_sum[:, wide:].T,
            vectors[5],
        )

    return body


def solution(mesh):
    placed = (
        P(("dp", "tensor"), None),
        P(("dp", "tensor"), None),
        P(),
        P(),
        P("dp", None, "tensor"),
        P(None, "tensor"),
        P("tensor", "dp"),
        P(),
        P(),
        P(),
        P("dp", "tensor"),
        P("tensor"),
        P("tensor", "dp"),
        P(),
    )
    return jax.shard_map(
        make_body(mesh.shape["dp"], mesh.shape["tensor"]),
        mesh=mesh,
        in_specs=placed,
        out_specs=(
            P(("dp", "tensor"), None),
            P(("dp", "tensor"), None),
            P(),
            P(),
            P("dp", None, "tensor"),
            P(None, "tensor"),
            P("tensor", "dp"),
            P(),
            P(),
            P(),
            P("dp", "tensor"),
            P("tensor"),
            P("tensor", "dp"),
            P(),
        ),
        check_vma=False,
    )
```

```python
import functools
import math

import jax
import jax.numpy as jnp
from jax import lax
from jax.experimental import pallas as pl
from jax.experimental.pallas import tpu as pltpu
from jax.sharding import PartitionSpec as P

HEADS = 16
HEAD = 64
AXES = ("dp", "tensor")
LOW = jnp.bfloat16
WIDE = jnp.float32


def together(*values):
    return lax.optimization_barrier(values)


def stats(rows):
    average = jnp.mean(rows, axis=-1, keepdims=True)
    centered = rows - average
    variance = jnp.mean(centered * centered, axis=-1, keepdims=True)
    scale = lax.rsqrt(variance + 1e-05)
    return centered * scale, scale


def norm_back(grad, gain, unit, scale):
    inner = grad * gain
    first = jnp.mean(inner, axis=-1, keepdims=True)
    second = jnp.mean(inner * unit, axis=-1, keepdims=True)
    return scale * (inner - first - unit * second)


def gelu_local(hidden):
    return jax.nn.gelu(hidden, approximate=True)


def clean_dot(x, y, contract):
    return lax.dot_general(x, y, (contract, ((), ())), preferred_element_type=WIDE)


def row_norm(rows):
    centered = rows - jnp.mean(rows, axis=-1, keepdims=True)
    variance = jnp.mean(centered * centered, axis=-1, keepdims=True)
    return centered * lax.rsqrt(variance + 1e-05)


def distances(starts, rows):
    count = starts.shape[0]
    down = lax.broadcasted_iota(jnp.int32, (rows, 1), 0)
    across = lax.broadcasted_iota(jnp.int32, (1, rows), 1)
    down = jnp.concatenate([down + starts[k] for k in range(count)], axis=0)
    across = jnp.concatenate([across + starts[k] for k in range(count)], axis=1)
    return (across - down).astype(WIDE)


def attend_kernel(
    heads, slopes, starts, row_a, gain, shift, weights, bias, row_b, row_c, row_d,
    normed, mixed, context, totals, branch_a, branch_b, branch_c, branch_d, turned,
):
    rows = row_a.shape[0]
    local = heads * HEAD
    for k, block in enumerate((row_a, row_b, row_c, row_d)):
        unit = row_norm(block[...].astype(WIDE))
        low = (unit * gain[...] + shift[...]).astype(LOW)
        here = pl.ds(k * rows, rows)
        normed[here, :] = low
        out = jnp.dot(low, weights[:, : 3 * local], preferred_element_type=WIDE)
        mixed[here, :] = (out + bias[...]).astype(LOW)
    distance = distances(starts, rows)
    allowed = distance >= 0
    for h in range(heads):
        query = mixed[:, pl.ds(h * HEAD, HEAD)]
        key = mixed[:, pl.ds(local + h * HEAD, HEAD)]
        value = mixed[:, pl.ds(2 * local + h * HEAD, HEAD)]
        scores = clean_dot(key, query, ((1,), (1,))) * HEAD ** (-0.5) - slopes[h] * distance
        scores = jnp.where(allowed, scores, -1e30)
        top = jnp.max(scores, axis=0, keepdims=True)
        grown = jnp.exp(scores - top)
        total = jnp.sum(grown, axis=0, keepdims=True)
        totals[h : h + 1, :] = top + jnp.log(total)
        soft = (grown * (1.0 / total)).astype(LOW)
        turned[h * HEAD : (h + 1) * HEAD, :] = jnp.dot(
            value.T, soft, preferred_element_type=WIDE
        ).astype(LOW)
    context[...] = turned[...].T
    for k, block in enumerate((branch_a, branch_b, branch_c, branch_d)):
        out = clean_dot(context[pl.ds(k * rows, rows), :], weights[:, 3 * local :], ((1,), (1,)))
        block[...] = out.astype(block.dtype)


def attend_back_kernel(
    heads, slopes, starts, grad_a, weights, grad_b, grad_c, grad_d, mixed, totals,
    row_a, row_b, row_c, row_d,
    mixed_grad, first_a, first_b, first_c, first_d, sums, vectors, back, turned,
):
    rows = row_a.shape[0]
    local = heads * HEAD
    for k, block in enumerate((grad_a, grad_b, grad_c, grad_d)):
        out = jnp.dot(block[...], weights[:, 3 * local :], preferred_element_type=WIDE)
        back[pl.ds(k * rows, rows), :] = out.astype(LOW)
    distance = distances(starts, rows)
    allowed = distance >= 0
    for h in range(heads):
        query = mixed[:, pl.ds(h * HEAD, HEAD)]
        key = mixed[:, pl.ds(local + h * HEAD, HEAD)]
        value = mixed[:, pl.ds(2 * local + h * HEAD, HEAD)]
        given = back[:, pl.ds(h * HEAD, HEAD)]
        scores = clean_dot(key, query, ((1,), (1,))) * HEAD ** (-0.5) - slopes[h] * distance
        scores = jnp.where(allowed, scores, -1e30)
        soft = jnp.exp(scores - totals[h : h + 1, :])
        value_grad = jnp.dot(soft.astype(LOW), given, preferred_element_type=WIDE)
        soft_grad = clean_dot(value, given, ((1,), (1,)))
        middle = jnp.sum(soft * soft_grad, axis=0, keepdims=True)
        score_grad = (soft * (soft_grad - middle)).astype(LOW)
        key_grad = jnp.dot(score_grad, query, preferred_element_type=WIDE) * HEAD ** (-0.5)
        query_grad = jnp.dot(key.T, score_grad, preferred_element_type=WIDE) * HEAD ** (-0.5)
        turned[h * HEAD : (h + 1) * HEAD, :] = query_grad.astype(LOW)
        mixed_grad[:, pl.ds(local + h * HEAD, HEAD)] = key_grad.astype(LOW)
        mixed_grad[:, pl.ds(2 * local + h * HEAD, HEAD)] = value_grad.astype(LOW)
    mixed_grad[:, :local] = turned[...].T
    sums[...] = jnp.sum(mixed_grad[...].astype(WIDE), axis=0, keepdims=True)
    gain_sum = jnp.zeros(vectors.shape[1:], WIDE)[None]
    shift_sum = gain_sum
    for k, (block, unit) in enumerate(
        ((first_a, row_a), (first_b, row_b), (first_c, row_c), (first_d, row_d))
    ):
        here = mixed_grad[pl.ds(k * rows, rows), :]
        out = clean_dot(here, weights[:, : 3 * local], ((1,), (1,)))
        block[...] = out.astype(block.dtype)
        unit = row_norm(unit[...].astype(WIDE))
        gain_sum = gain_sum + jnp.sum(out * unit, axis=0, keepdims=True)
        shift_sum = shift_sum + jnp.sum(out, axis=0, keepdims=True)
    vectors[0:1, :] = gain_sum
    vectors[1:2, :] = shift_sum


def feed_kernel(
    row_a, expand, bias, top_a, shrink, row_b, top_b, row_c, top_c, row_d, top_d,
    active, back, part_a, part_b, part_c, part_d, sums,
):
    rows = row_a.shape[0]
    wide = active.shape[1]
    total = jnp.zeros((1, wide), WIDE)
    ins = ((row_a, top_a, part_a), (row_b, top_b, part_b), (row_c, top_c, part_c), (row_d, top_d, part_d))
    for k, (row, top, part) in enumerate(ins):
        here = pl.ds(k * rows, rows)
        hidden = jnp.dot(row[...], expand[...], preferred_element_type=WIDE) + bias[...]
        square = hidden * hidden
        curve = jnp.tanh(0.7978845608028654 * hidden * (1.0 + 0.044715 * square))
        half = 0.5 * (1.0 + curve)
        active[here, :] = (hidden * half).astype(LOW)
        slope = 0.7978845608028654 * (1.0 + 3 * 0.044715 * square)
        slope = half + 0.5 * hidden * (1.0 - curve * curve) * slope
        grad = jnp.dot(top[...], shrink[...], preferred_element_type=WIDE)
        grad = (grad * slope).astype(LOW)
        back[here, :] = grad
        total = total + jnp.sum(grad.astype(WIDE), axis=0, keepdims=True)
        out = clean_dot(grad, expand[...], ((1,), (1,)))
        part[...] = out.astype(part.dtype)
    sums[...] = total


class Late:
    def __init__(self, copy, ref):
        self.copy, self.ref, self.shape = copy, ref, ref.shape

    def here(self):
        if self.copy is not None:
            self.copy.wait()
            self.copy = None
        return self.ref

    def __getitem__(self, index):
        return self.here()[index]


def call_kernel(body, scalars, arrays, outs, scratch, flops, mega=32):
    count, first = len(arrays), len(scalars)

    def kernel(*refs):
        sources = refs[first : first + count]
        results = refs[first + count : first + count + len(outs)]
        rest = refs[first + count + len(outs) :]
        held, arrived, own = rest[:count], rest[count], rest[count + 1 :]
        inputs = []
        for k in range(count):
            copy = pltpu.make_async_copy(sources[k], held[k], arrived.at[k])
            copy.start()
            inputs.append(Late(copy, held[k]))
        body(*refs[:first], *inputs, *results, *own)
        for late in inputs:
            late.here()

    def space(array):
        return pl.BlockSpec(array.shape, lambda _: (0,) * len(array.shape))

    sizes = sum(math.prod(a.shape) * a.dtype.itemsize for a in list(arrays) + list(outs))
    return pl.pallas_call(
        kernel,
        grid=(1,),
        in_specs=[pl.BlockSpec(memory_space=pltpu.SMEM)] * first
        + [pl.BlockSpec(memory_space=pltpu.HBM)] * count,
        out_specs=[space(array) for array in outs],
        out_shape=outs,
        scratch_shapes=[pltpu.VMEM(array.shape, array.dtype) for array in arrays]
        + [pltpu.SemaphoreType.DMA((count,))]
        + scratch,
        compiler_params=pltpu.CompilerParams(vmem_limit_bytes=mega << 20),
        cost_estimate=pl.CostEstimate(flops=flops, bytes_accessed=sizes, transcendentals=0),
    )(*scalars, *arrays)


def grads_kernel(steps, x_ref, y_ref, u_ref, v_ref, out_ref, turned):
    step = pl.program_id(0)

    @pl.when(step == 0)
    def _():
        turned[...] = x_ref[...].T

    @pl.when(step == steps)
    def _():
        turned[...] = u_ref[...].T

    @pl.when(step < steps)
    def _():
        out = jnp.dot(turned[...], y_ref[...], preferred_element_type=WIDE)
        out_ref[...] = out.astype(LOW)

    @pl.when(step >= steps)
    def _():
        out = jnp.dot(turned[...], v_ref[...], preferred_element_type=WIDE)
        out_ref[...] = out.astype(LOW)


def weight_grads(x, y, u, v):
    tokens, width = x.shape
    columns = 256
    steps, more = y.shape[1] // columns, v.shape[1] // columns
    whole = pl.BlockSpec((tokens, width), lambda j: (0, 0))
    return pl.pallas_call(
        functools.partial(grads_kernel, steps),
        grid=(steps + more,),
        in_specs=[
            whole,
            pl.BlockSpec((tokens, columns), lambda j: (0, jnp.minimum(j, steps - 1))),
            whole,
            pl.BlockSpec((tokens, columns), lambda j: (0, jnp.maximum(j - steps, 0))),
        ],
        out_specs=pl.BlockSpec((width, columns), lambda j: (0, j)),
        out_shape=jax.ShapeDtypeStruct((width, columns * (steps + more)), LOW),
        scratch_shapes=[pltpu.VMEM((width, tokens), LOW)],
        compiler_params=pltpu.CompilerParams(vmem_limit_bytes=24 << 20),
        cost_estimate=pl.CostEstimate(
            flops=2 * tokens * width * columns * (steps + more),
            bytes_accessed=2 * width * (2 * tokens + columns * (steps + more)),
            transcendentals=0,
        ),
    )(x, y, u, v)


def make_body(n_dp, n_t):
    bits = [1 << k for k in range(1, n_dp.bit_length() - 1)]

    def send(value, target, name):
        pairs = []
        for d in range(n_dp):
            for t in range(n_t):
                goal = target(d, t)
                if goal is not None:
                    pairs.append((d * n_t + t, goal[0] * n_t + goal[1]))
        with jax.named_scope(name):
            return lax.ppermute(value, AXES, pairs)

    def swap_z(value, mask, name):
        return send(value, lambda d, t: (d, t ^ mask), f"{name}_z{mask}")

    def swap_dp(value, mask, name):
        return send(value, lambda d, t: (d ^ mask, t), f"{name}_d{mask}")

    def bit_of(mask):
        return (lax.axis_index("dp") & mask) != 0

    class Spread:
        def __init__(self, first, second, name):
            lead = (1,) * len(bits)
            self.ops = [first.reshape(lead + first.shape), second.reshape(lead + second.shape)]
            self.shapes = (first.shape, second.shape)
            self.name = name
            self.left = list(zip(bits[::-1], bits))

        def go(self):
            self.masks = self.left.pop(0)
            self.others = [
                swap_dp(value, mask, self.name + label)
                for value, mask, label in zip(self.ops, self.masks, ("_a", "_b"))
            ]

        def land(self):
            for k, (mask, other) in enumerate(zip(self.masks, self.others)):
                axis = len(bits) - 1 - bits.index(mask)
                own, flag = self.ops[k], bit_of(mask)
                self.ops[k] = jnp.concatenate(
                    [jnp.where(flag, other, own), jnp.where(flag, own, other)], axis=axis
                )

        def finish(self):
            while self.left:
                self.go()
                self.land()
                self.ops = list(together(*self.ops))
            return [
                value.reshape((-1,) + shape[1:]) for value, shape in zip(self.ops, self.shapes)
            ]

    class Fold:
        def __init__(self, first, second, name):
            lead = (2,) * len(bits)
            self.shapes = (first.shape, second.shape)
            self.values = [
                first.reshape(lead + first.shape[1:]),
                second.reshape(lead + second.shape[1:]),
            ]
            self.name = name
            self.left = list(zip(bits, bits[::-1]))
            self.cut()

        def cut(self):
            self.ops, self.keep = [], []
            for value, mask in zip(self.values, self.left[0]):
                axis = len(bits) - 1 - bits.index(mask)
                place = (lax.axis_index("dp") // mask) % 2
                self.keep.append(lax.dynamic_slice_in_dim(value, place, 1, axis))
                self.ops.append(lax.dynamic_slice_in_dim(value, 1 - place, 1, axis).astype(LOW))

        def go(self):
            masks = self.left.pop(0)
            self.others = [
                swap_dp(value, mask, self.name + label)
                for value, mask, label in zip(self.ops, masks, ("_a", "_b"))
            ]

        def land(self):
            self.values = [
                (keep.astype(WIDE) + other.astype(WIDE)).astype(LOW)
                for keep, other in zip(self.keep, self.others)
            ]
            self.ops = list(self.values)
            if self.left:
                self.cut()

        def finish(self):
            while self.left:
                self.go()
                self.land()
                self.ops = list(together(*self.ops))
            return [value.reshape(shape[1:]) for value, shape in zip(self.ops, self.shapes)]

    def gate(chain, *values):
        count = len(chain.ops)
        *ops, = together(*chain.ops, *values)
        chain.ops = ops[:count]
        return ops[count:]

    def gather_z(value, name):
        one = swap_z(value, 1, name)
        two = swap_z(value, 2, name)
        return [value, one, two, swap_z(two, 1, name + "_far")]

    def fold_far(parts, name):
        far = swap_z(parts[3].astype(LOW), 1, name + "_far")
        return (parts[2].astype(WIDE) + far.astype(WIDE)).astype(LOW)

    def fold_near(parts, both, name):
        two = swap_z(both, 2, name)
        one = swap_z(parts[1].astype(LOW), 1, name)
        return one, two

    def fold_end(parts, one, two):
        return parts[0].astype(WIDE) + one.astype(WIDE) + two.astype(WIDE)

    def body(
        block_input,
        output_cotangent,
        first_gain,
        first_shift,
        project_in,
        query_value_bias,
        project_out,
        project_out_bias,
        second_gain,
        second_shift,
        expand_weight,
        expand_bias,
        shrink_weight,
        shrink_bias,
    ):
        rows, width = block_input.shape
        local = project_out.shape[0]
        wide = expand_weight.shape[1]
        heads = local // HEAD
        core = lax.axis_index("dp") % 2
        place = lax.axis_index("tensor")
        gain_one, shift_one = first_gain.astype(WIDE), first_shift.astype(WIDE)
        gain_two, shift_two = second_gain.astype(WIDE), second_shift.astype(WIDE)
        bias_qv = query_value_bias.astype(WIDE)
        tokens = n_t * rows

        def shape(*dims, kind=WIDE):
            return jax.ShapeDtypeStruct(dims, kind)

        def parts():
            return [shape(rows, width)] + [shape(rows, width, kind=LOW)] * (n_t - 1)


        part_in = project_in.reshape(project_in.shape[0], 3 * local)
        part_a = part_in[:, : 2 * local]
        part_b = jnp.concatenate([part_in[:, 2 * local :], project_out.T], axis=1)
        rows_one = swap_z(block_input, 1, "rows")
        rows_two = swap_z(block_input, 2, "rows")
        attend = Spread(part_a[None], part_b[None], "att")
        attend.go()
        attend.land()
        (rows_one,) = gate(attend, rows_one)
        while len(attend.left) > 1:
            attend.go()
            attend.land()
        attend.go()
        attend.land()
        near = jnp.concatenate([expand_weight, shrink_weight.T], axis=1)
        rows_two, near = gate(attend, rows_two, near)
        rows_three = swap_z(rows_two, 1, "rows_far")
        full_a, full_b = attend.finish()
        pair = jnp.concatenate([full_a, full_b], axis=-1)
        mate = swap_dp(pair, 1, "att")
        full = jnp.stack([jnp.where(core == 0, pair, mate), jnp.where(core == 0, mate, pair)], 1)
        full = full.reshape(width, 4 * local)
        full, near, top_low, rows_three = together(full, near, output_cotangent, rows_three)
        rows_list = [block_input, rows_one, rows_two, rows_three]

        feed = lax.all_gather(near, "dp", axis=0, tiled=True)
        bias_wide = expand_bias.astype(WIDE)
        full_expand, full_shrink = feed[:, :wide], feed[:, wide:]

        bias_full = jnp.concatenate([bias_qv[0], jnp.zeros_like(bias_qv[0]), bias_qv[1]])
        starts = ((jnp.arange(n_t) ^ place) * rows).astype(jnp.int32)
        head_ids = (place * heads + jnp.arange(heads) + 1).astype(WIDE)
        slopes = jnp.exp2(-8.0 * head_ids / HEADS)
        normed_all, mixed, context, totals, *branch_low = call_kernel(
            functools.partial(attend_kernel, heads),
            [slopes, starts],
            [rows_list[0], gain_one[None], shift_one[None], full, bias_full[None]]
            + rows_list[1:],
            [
                shape(tokens, width, kind=LOW),
                shape(tokens, 3 * local, kind=LOW),
                shape(tokens, local, kind=LOW),
                shape(heads, tokens),
            ]
            + parts(),
            [pltpu.VMEM((local, tokens), LOW)],
            2 * tokens * width * 4 * local + 4 * tokens * tokens * local,
        )
        tops_one, tops_two = swap_z(top_low, 1, "tops"), swap_z(top_low, 2, "tops")
        both = fold_far(branch_low, "branch")
        both, tops_one, tops_two, branch_low[1] = together(both, tops_one, tops_two, branch_low[1])
        tops_far = swap_z(tops_two, 1, "tops_far")
        one, two = fold_near(branch_low, both, "branch")
        one, two, tops_far = together(one, two, tops_far)
        tops_list = [top_low, tops_one, tops_two, tops_far]
        branch = fold_end(branch_low, one, two)
        middle = block_input.astype(WIDE) + branch + project_out_bias.astype(WIDE)

        unit_two, scale_two = stats(middle)
        second_low = (unit_two * gain_two + shift_two).astype(LOW)
        second_list = gather_z(second_low, "second")
        active, hidden_grad, *second_parts, expand_bias_part = call_kernel(
            feed_kernel,
            [],
            [second_list[0], full_expand, bias_wide[None], tops_list[0], full_shrink]
            + [block for two in zip(second_list[1:], tops_list[1:]) for block in two],
            [shape(tokens, wide, kind=LOW), shape(tokens, wide, kind=LOW)]
            + parts()
            + [shape(1, wide)],
            [],
            6 * tokens * width * wide,
        )
        second_low_parts = second_parts
        both = fold_far(second_low_parts, "second_grad")
        second_all = jnp.concatenate(second_list, axis=0)
        tops = jnp.concatenate(tops_list, axis=0)
        feed_grad = weight_grads(second_all, hidden_grad, tops, active)
        both, feed_grad = together(both, feed_grad)
        shrunk = jnp.einsum("sf,df->sd", active, full_shrink, preferred_element_type=WIDE)
        shrunk = shrunk.reshape(n_t, rows, width)
        shrunk = [shrunk[0]] + [shrunk[k].astype(LOW) for k in range(1, n_t)]
        second_grad = fold_end(second_low_parts, *fold_near(second_low_parts, both, "second_grad"))
        feed_sum = lax.psum_scatter(feed_grad, "dp", scatter_dimension=0, tiled=True)
        feed_sum = feed_sum.astype(WIDE)
        upstream = output_cotangent.astype(WIDE)
        middle_grad = upstream + norm_back(second_grad, gain_two, unit_two, scale_two)
        middle_list = gather_z(middle_grad.astype(LOW), "middle")
        *middle_list, shrunk[1], shrunk[2], shrunk[3] = together(*middle_list, *shrunk[1:])
        shrunk_both = fold_far(shrunk, "shrunk")

        middle_all = jnp.concatenate(middle_list, axis=0)
        mixed_grad, *first_low, mixed_sums, gain_parts = call_kernel(
            functools.partial(attend_back_kernel, heads),
            [slopes, starts],
            [middle_list[0], full] + middle_list[1:] + [mixed, totals] + rows_list,
            [shape(tokens, 3 * local, kind=LOW)]
            + parts()
            + [shape(1, 3 * local), shape(2, width)],
            [pltpu.VMEM((tokens, local), LOW), pltpu.VMEM((local, tokens), LOW)],
            2 * tokens * width * 4 * local + 10 * tokens * tokens * local,
        )
        mixed_sums = mixed_sums[0]
        shrunk_one, shrunk_two = fold_near(shrunk, shrunk_both, "shrunk")
        both = fold_far(first_low, "first_grad")
        grads = weight_grads(normed_all, mixed_grad, middle_all, context)
        both, grads, shrunk_one, shrunk_two, feed_sum = together(
            both, grads, shrunk_one, shrunk_two, feed_sum
        )
        grads = lax.psum_scatter(grads, "dp", scatter_dimension=0, tiled=True).astype(WIDE)
        in_sum, out_sum = grads[:, : 3 * local], grads[:, 3 * local :].T
        result = middle + fold_end(shrunk, shrunk_one, shrunk_two) + shrink_bias.astype(WIDE)
        result = result.astype(LOW)
        first_one, first_two = fold_near(first_low, both, "first_grad")
        first_one, first_two, gain_parts = together(first_one, first_two, gain_parts)
        first_grad = fold_end(first_low, first_one, first_two)

        unit, scale = stats(block_input.astype(WIDE))
        input_grad = middle_grad + norm_back(first_grad, gain_one, unit, scale)
        slot = jnp.arange(n_t)[:, None]
        bias_slots = jnp.where(slot == place, expand_bias_part, 0.0)
        qv_parts = jnp.stack([mixed_sums[:local], mixed_sums[2 * local :]])
        qv_slots = jnp.where(slot[None] == place, qv_parts[:, None], 0.0)
        vectors = jnp.concatenate(
            [
                jnp.stack(
                    [
                        gain_parts[0],
                        gain_parts[1],
                        jnp.sum(middle_grad, axis=0),
                        jnp.sum(second_grad * unit_two, axis=0),
                        jnp.sum(second_grad, axis=0),
                        jnp.sum(upstream, axis=0),
                    ]
                ),
                bias_slots.reshape(-1, width),
                qv_slots.reshape(2, -1),
            ],
            axis=0,
        )
        for mask in [1] + bits:
            vectors = vectors + swap_dp(vectors, mask, "vectors")
        for mask in (1, 2):
            vectors = vectors + swap_z(vectors, mask, "vectors")
        bias_slots = vectors[6:-2].reshape(n_t, wide)
        expand_bias_sum = lax.dynamic_index_in_dim(bias_slots, place, 0, keepdims=False)
        qv_slots = vectors[-2:].reshape(2, n_t, local)
        qv_sum = lax.dynamic_index_in_dim(qv_slots, place, 1, keepdims=False)
        return (
            result,
            input_grad.astype(LOW),
            vectors[0],
            vectors[1],
            in_sum.reshape(project_in.shape),
            qv_sum,
            out_sum,
            vectors[2],
            vectors[3],
            vectors[4],
            feed_sum[:, :wide],
            expand_bias_sum,
            feed_sum[:, wide:].T,
            vectors[5],
        )

    return body


def solution(mesh):
    placed = (
        P(("dp", "tensor"), None),
        P(("dp", "tensor"), None),
        P(),
        P(),
        P("dp", None, "tensor"),
        P(None, "tensor"),
        P("tensor", "dp"),
        P(),
        P(),
        P(),
        P("dp", "tensor"),
        P("tensor"),
        P("tensor", "dp"),
        P(),
    )
    return jax.shard_map(
        make_body(mesh.shape["dp"], mesh.shape["tensor"]),
        mesh=mesh,
        in_specs=placed,
        out_specs=(
            P(("dp", "tensor"), None),
            P(("dp", "tensor"), None),
            P(),
            P(),
            P("dp", None, "tensor"),
            P(None, "tensor"),
            P("tensor", "dp"),
            P(),
            P(),
            P(),
            P("dp", "tensor"),
            P("tensor"),
            P("tensor", "dp"),
            P(),
        ),
        check_vma=False,
    )
```

```python
import functools
import math

import jax
import jax.numpy as jnp
from jax import lax
from jax.experimental import pallas as pl
from jax.experimental.pallas import tpu as pltpu
from jax.sharding import PartitionSpec as P

HEADS = 16
HEAD = 64
AXES = ("dp", "tensor")
LOW = jnp.bfloat16
WIDE = jnp.float32


def together(*values):
    return lax.optimization_barrier(values)


def stats(rows):
    average = jnp.mean(rows, axis=-1, keepdims=True)
    centered = rows - average
    variance = jnp.mean(centered * centered, axis=-1, keepdims=True)
    scale = lax.rsqrt(variance + 1e-05)
    return centered * scale, scale


def norm_back(grad, gain, unit, scale):
    inner = grad * gain
    first = jnp.mean(inner, axis=-1, keepdims=True)
    second = jnp.mean(inner * unit, axis=-1, keepdims=True)
    return scale * (inner - first - unit * second)


def gelu_local(hidden):
    return jax.nn.gelu(hidden, approximate=True)


def clean_dot(x, y, contract):
    return lax.dot_general(x, y, (contract, ((), ())), preferred_element_type=WIDE)


def row_norm(rows):
    centered = rows - jnp.mean(rows, axis=-1, keepdims=True)
    variance = jnp.mean(centered * centered, axis=-1, keepdims=True)
    return centered * lax.rsqrt(variance + 1e-05)


def distances(starts, rows):
    count = starts.shape[0]
    down = lax.broadcasted_iota(jnp.int32, (rows, 1), 0)
    across = lax.broadcasted_iota(jnp.int32, (1, rows), 1)
    down = jnp.concatenate([down + starts[k] for k in range(count)], axis=0)
    across = jnp.concatenate([across + starts[k] for k in range(count)], axis=1)
    return (across - down).astype(WIDE)


def attend_kernel(
    heads, slopes, starts, row_a, gain, shift, weights, bias, row_b, row_c, row_d,
    normed, mixed, context, totals, branch_a, branch_b, branch_c, branch_d, turned,
):
    rows = row_a.shape[0]
    local = heads * HEAD
    for k, block in enumerate((row_a, row_b, row_c, row_d)):
        unit = row_norm(block[...].astype(WIDE))
        low = (unit * gain[...] + shift[...]).astype(LOW)
        here = pl.ds(k * rows, rows)
        normed[here, :] = low
        out = jnp.dot(low, weights[:, : 3 * local], preferred_element_type=WIDE)
        mixed[here, :] = (out + bias[...]).astype(LOW)
    distance = distances(starts, rows)
    allowed = distance >= 0
    for h in range(heads):
        query = mixed[:, pl.ds(h * HEAD, HEAD)]
        key = mixed[:, pl.ds(local + h * HEAD, HEAD)]
        value = mixed[:, pl.ds(2 * local + h * HEAD, HEAD)]
        scores = clean_dot(key, query, ((1,), (1,))) * HEAD ** (-0.5) - slopes[h] * distance
        scores = jnp.where(allowed, scores, -1e30)
        top = jnp.max(scores, axis=0, keepdims=True)
        grown = jnp.exp(scores - top)
        total = jnp.sum(grown, axis=0, keepdims=True)
        totals[h : h + 1, :] = top + jnp.log(total)
        soft = (grown * (1.0 / total)).astype(LOW)
        turned[h * HEAD : (h + 1) * HEAD, :] = jnp.dot(
            value.T, soft, preferred_element_type=WIDE
        ).astype(LOW)
    context[...] = turned[...].T
    for k, block in enumerate((branch_a, branch_b, branch_c, branch_d)):
        out = clean_dot(context[pl.ds(k * rows, rows), :], weights[:, 3 * local :], ((1,), (1,)))
        block[...] = out.astype(block.dtype)


def attend_back_kernel(
    heads, slopes, starts, grad_a, weights, grad_b, grad_c, grad_d, mixed, totals,
    row_a, row_b, row_c, row_d,
    mixed_grad, first_a, first_b, first_c, first_d, sums, vectors, back, turned,
):
    rows = row_a.shape[0]
    local = heads * HEAD
    for k, block in enumerate((grad_a, grad_b, grad_c, grad_d)):
        out = jnp.dot(block[...], weights[:, 3 * local :], preferred_element_type=WIDE)
        back[pl.ds(k * rows, rows), :] = out.astype(LOW)
    distance = distances(starts, rows)
    allowed = distance >= 0
    for h in range(heads):
        query = mixed[:, pl.ds(h * HEAD, HEAD)]
        key = mixed[:, pl.ds(local + h * HEAD, HEAD)]
        value = mixed[:, pl.ds(2 * local + h * HEAD, HEAD)]
        given = back[:, pl.ds(h * HEAD, HEAD)]
        scores = clean_dot(key, query, ((1,), (1,))) * HEAD ** (-0.5) - slopes[h] * distance
        scores = jnp.where(allowed, scores, -1e30)
        soft = jnp.exp(scores - totals[h : h + 1, :])
        value_grad = jnp.dot(soft.astype(LOW), given, preferred_element_type=WIDE)
        soft_grad = clean_dot(value, given, ((1,), (1,)))
        middle = jnp.sum(soft * soft_grad, axis=0, keepdims=True)
        score_grad = (soft * (soft_grad - middle)).astype(LOW)
        key_grad = jnp.dot(score_grad, query, preferred_element_type=WIDE) * HEAD ** (-0.5)
        query_grad = jnp.dot(key.T, score_grad, preferred_element_type=WIDE) * HEAD ** (-0.5)
        turned[h * HEAD : (h + 1) * HEAD, :] = query_grad.astype(LOW)
        mixed_grad[:, pl.ds(local + h * HEAD, HEAD)] = key_grad.astype(LOW)
        mixed_grad[:, pl.ds(2 * local + h * HEAD, HEAD)] = value_grad.astype(LOW)
    mixed_grad[:, :local] = turned[...].T
    sums[...] = jnp.sum(mixed_grad[...].astype(WIDE), axis=0, keepdims=True)
    gain_sum = jnp.zeros(vectors.shape[1:], WIDE)[None]
    shift_sum = gain_sum
    for k, (block, unit) in enumerate(
        ((first_a, row_a), (first_b, row_b), (first_c, row_c), (first_d, row_d))
    ):
        here = mixed_grad[pl.ds(k * rows, rows), :]
        out = clean_dot(here, weights[:, : 3 * local], ((1,), (1,)))
        block[...] = out.astype(block.dtype)
        unit = row_norm(unit[...].astype(WIDE))
        gain_sum = gain_sum + jnp.sum(out * unit, axis=0, keepdims=True)
        shift_sum = shift_sum + jnp.sum(out, axis=0, keepdims=True)
    vectors[0:1, :] = gain_sum
    vectors[1:2, :] = shift_sum


def feed_kernel(
    row_a, weights, bias, top_a, row_b, top_b, row_c, top_c, row_d, top_d,
    active, back, part_a, part_b, part_c, part_d, sums,
):
    rows = row_a.shape[0]
    wide = active.shape[1]
    total = jnp.zeros((1, wide), WIDE)
    ins = ((row_a, top_a, part_a), (row_b, top_b, part_b), (row_c, top_c, part_c), (row_d, top_d, part_d))
    for k, (row, top, part) in enumerate(ins):
        here = pl.ds(k * rows, rows)
        hidden = jnp.dot(row[...], weights[:, :wide], preferred_element_type=WIDE) + bias[...]
        square = hidden * hidden
        curve = jnp.tanh(0.7978845608028654 * hidden * (1.0 + 0.044715 * square))
        half = 0.5 * (1.0 + curve)
        active[here, :] = (hidden * half).astype(LOW)
        slope = 0.7978845608028654 * (1.0 + 3 * 0.044715 * square)
        slope = half + 0.5 * hidden * (1.0 - curve * curve) * slope
        grad = jnp.dot(top[...], weights[:, wide:], preferred_element_type=WIDE)
        grad = (grad * slope).astype(LOW)
        back[here, :] = grad
        total = total + jnp.sum(grad.astype(WIDE), axis=0, keepdims=True)
        out = clean_dot(grad, weights[:, :wide], ((1,), (1,)))
        part[...] = out.astype(part.dtype)
    sums[...] = total


class Late:
    def __init__(self, copy, ref):
        self.copy, self.ref, self.shape = copy, ref, ref.shape

    def here(self):
        if self.copy is not None:
            self.copy.wait()
            self.copy = None
        return self.ref

    def __getitem__(self, index):
        return self.here()[index]


def call_kernel(body, scalars, arrays, outs, scratch, flops, mega=32):
    count, first = len(arrays), len(scalars)

    def kernel(*refs):
        sources = refs[first : first + count]
        results = refs[first + count : first + count + len(outs)]
        rest = refs[first + count + len(outs) :]
        held, arrived, own = rest[:count], rest[count], rest[count + 1 :]
        inputs = []
        for k in range(count):
            copy = pltpu.make_async_copy(sources[k], held[k], arrived.at[k])
            copy.start()
            inputs.append(Late(copy, held[k]))
        body(*refs[:first], *inputs, *results, *own)
        for late in inputs:
            late.here()

    def space(array):
        return pl.BlockSpec(array.shape, lambda _: (0,) * len(array.shape))

    sizes = sum(math.prod(a.shape) * a.dtype.itemsize for a in list(arrays) + list(outs))
    return pl.pallas_call(
        kernel,
        grid=(1,),
        in_specs=[pl.BlockSpec(memory_space=pltpu.SMEM)] * first
        + [pl.BlockSpec(memory_space=pltpu.HBM)] * count,
        out_specs=[space(array) for array in outs],
        out_shape=outs,
        scratch_shapes=[pltpu.VMEM(array.shape, array.dtype) for array in arrays]
        + [pltpu.SemaphoreType.DMA((count,))]
        + scratch,
        compiler_params=pltpu.CompilerParams(vmem_limit_bytes=mega << 20),
        cost_estimate=pl.CostEstimate(flops=flops, bytes_accessed=sizes, transcendentals=0),
    )(*scalars, *arrays)


def grads_kernel(steps, count, *refs):
    blocks, others = refs[:count], refs[count + 1 : -4]
    y_ref, v_ref, out_ref, more_ref, turned = refs[count], *refs[-4:]
    step = pl.program_id(0)

    def turn(pieces):
        first = 0
        for piece in pieces:
            size = piece.shape[0]
            turned[:, first : first + size] = piece[...].T
            first += size

    @pl.when(step == 0)
    def _():
        turn(blocks)

    @pl.when(step == steps)
    def _():
        turn(others)

    @pl.when(step < steps)
    def _():
        out = jnp.dot(turned[...], y_ref[...], preferred_element_type=WIDE)
        out_ref[...] = out.astype(LOW)

    @pl.when(step >= steps)
    def _():
        out = jnp.dot(turned[...], v_ref[...], preferred_element_type=WIDE)
        more_ref[...] = out.astype(LOW)


def weight_grads(blocks, y, others, v):
    tokens, width = y.shape[0], blocks[0].shape[1]
    columns = 256
    steps, more = y.shape[1] // columns, v.shape[1] // columns

    def whole(block):
        return pl.BlockSpec(block.shape, lambda j: (0, 0))

    return pl.pallas_call(
        functools.partial(grads_kernel, steps, len(blocks)),
        grid=(steps + more,),
        in_specs=[whole(block) for block in blocks]
        + [pl.BlockSpec((tokens, columns), lambda j: (0, jnp.minimum(j, steps - 1)))]
        + [whole(block) for block in others]
        + [pl.BlockSpec((tokens, columns), lambda j: (0, jnp.maximum(j - steps, 0)))],
        out_specs=[
            pl.BlockSpec((width, columns), lambda j: (0, jnp.minimum(j, steps - 1))),
            pl.BlockSpec((width, columns), lambda j: (0, jnp.maximum(j - steps, 0))),
        ],
        out_shape=[jax.ShapeDtypeStruct((width, z.shape[1]), LOW) for z in (y, v)],
        scratch_shapes=[pltpu.VMEM((width, tokens), LOW)],
        compiler_params=pltpu.CompilerParams(vmem_limit_bytes=24 << 20),
        cost_estimate=pl.CostEstimate(
            flops=2 * tokens * width * columns * (steps + more),
            bytes_accessed=2 * width * (2 * tokens + columns * (steps + more)),
            transcendentals=0,
        ),
    )(*blocks, y, *others, v)


def make_body(n_dp, n_t):
    bits = [1 << k for k in range(1, n_dp.bit_length() - 1)]

    def send(value, target, name):
        pairs = []
        for d in range(n_dp):
            for t in range(n_t):
                goal = target(d, t)
                if goal is not None:
                    pairs.append((d * n_t + t, goal[0] * n_t + goal[1]))
        with jax.named_scope(name):
            return lax.ppermute(value, AXES, pairs)

    def swap_z(value, mask, name):
        return send(value, lambda d, t: (d, t ^ mask), f"{name}_z{mask}")

    def swap_dp(value, mask, name):
        return send(value, lambda d, t: (d ^ mask, t), f"{name}_d{mask}")

    def bit_of(mask):
        return (lax.axis_index("dp") & mask) != 0

    class Spread:
        def __init__(self, first, second, name):
            lead = (1,) * len(bits)
            self.ops = [first.reshape(lead + first.shape), second.reshape(lead + second.shape)]
            self.shapes = (first.shape, second.shape)
            self.name = name
            self.left = list(zip(bits[::-1], bits))

        def go(self):
            self.masks = self.left.pop(0)
            self.others = [
                swap_dp(value, mask, self.name + label)
                for value, mask, label in zip(self.ops, self.masks, ("_a", "_b"))
            ]

        def land(self):
            for k, (mask, other) in enumerate(zip(self.masks, self.others)):
                axis = len(bits) - 1 - bits.index(mask)
                own, flag = self.ops[k], bit_of(mask)
                self.ops[k] = jnp.concatenate(
                    [jnp.where(flag, other, own), jnp.where(flag, own, other)], axis=axis
                )

        def finish(self):
            while self.left:
                self.go()
                self.land()
                self.ops = list(together(*self.ops))
            return [
                value.reshape((-1,) + shape[1:]) for value, shape in zip(self.ops, self.shapes)
            ]

    class Fold:
        def __init__(self, first, second, name):
            lead = (2,) * len(bits)
            self.shapes = (first.shape, second.shape)
            self.values = [
                first.reshape(lead + first.shape[1:]),
                second.reshape(lead + second.shape[1:]),
            ]
            self.name = name
            self.left = list(zip(bits, bits[::-1]))
            self.cut()

        def cut(self):
            self.ops, self.keep = [], []
            for value, mask in zip(self.values, self.left[0]):
                axis = len(bits) - 1 - bits.index(mask)
                place = (lax.axis_index("dp") // mask) % 2
                self.keep.append(lax.dynamic_slice_in_dim(value, place, 1, axis))
                self.ops.append(lax.dynamic_slice_in_dim(value, 1 - place, 1, axis).astype(LOW))

        def go(self):
            masks = self.left.pop(0)
            self.others = [
                swap_dp(value, mask, self.name + label)
                for value, mask, label in zip(self.ops, masks, ("_a", "_b"))
            ]

        def land(self):
            self.values = [
                (keep.astype(WIDE) + other.astype(WIDE)).astype(LOW)
                for keep, other in zip(self.keep, self.others)
            ]
            self.ops = list(self.values)
            if self.left:
                self.cut()

        def finish(self):
            while self.left:
                self.go()
                self.land()
                self.ops = list(together(*self.ops))
            return [value.reshape(shape[1:]) for value, shape in zip(self.ops, self.shapes)]

    def gate(chain, *values):
        count = len(chain.ops)
        *ops, = together(*chain.ops, *values)
        chain.ops = ops[:count]
        return ops[count:]

    def gather_z(value, name):
        one = swap_z(value, 1, name)
        two = swap_z(value, 2, name)
        return [value, one, two, swap_z(two, 1, name + "_far")]

    def fold_far(parts, name):
        far = swap_z(parts[3].astype(LOW), 1, name + "_far")
        return (parts[2].astype(WIDE) + far.astype(WIDE)).astype(LOW)

    def fold_near(parts, both, name):
        two = swap_z(both, 2, name)
        one = swap_z(parts[1].astype(LOW), 1, name)
        return one, two

    def fold_end(parts, one, two):
        return parts[0].astype(WIDE) + one.astype(WIDE) + two.astype(WIDE)

    def body(
        block_input,
        output_cotangent,
        first_gain,
        first_shift,
        project_in,
        query_value_bias,
        project_out,
        project_out_bias,
        second_gain,
        second_shift,
        expand_weight,
        expand_bias,
        shrink_weight,
        shrink_bias,
    ):
        rows, width = block_input.shape
        local = project_out.shape[0]
        wide = expand_weight.shape[1]
        heads = local // HEAD
        core = lax.axis_index("dp") % 2
        place = lax.axis_index("tensor")
        gain_one, shift_one = first_gain.astype(WIDE), first_shift.astype(WIDE)
        gain_two, shift_two = second_gain.astype(WIDE), second_shift.astype(WIDE)
        bias_qv = query_value_bias.astype(WIDE)
        tokens = n_t * rows

        def shape(*dims, kind=WIDE):
            return jax.ShapeDtypeStruct(dims, kind)

        def parts():
            return [shape(rows, width)] + [shape(rows, width, kind=LOW)] * (n_t - 1)


        part_in = project_in.reshape(project_in.shape[0], 3 * local)
        part_a = part_in[:, : 2 * local]
        part_b = jnp.concatenate([part_in[:, 2 * local :], project_out.T], axis=1)
        near = jnp.concatenate([expand_weight, shrink_weight.T], axis=1)
        rows_one = swap_z(block_input, 1, "rows")
        rows_two = swap_z(block_input, 2, "rows")
        attend = Spread(part_a[None], part_b[None], "att")
        attend.go()
        attend.land()
        rows_one, rows_two, near = gate(attend, rows_one, rows_two, near)
        rows_three = swap_z(rows_two, 1, "rows_far")
        full_a, full_b = attend.finish()
        full_a, full_b, near, rows_three, top_low = together(
            full_a, full_b, near, rows_three, output_cotangent
        )
        pair = jnp.concatenate([full_a, full_b], axis=-1)
        mate = swap_dp(pair, 1, "att")
        full = jnp.stack([jnp.where(core == 0, pair, mate), jnp.where(core == 0, mate, pair)], 1)
        full = full.reshape(width, 4 * local)
        rows_list = [block_input, rows_one, rows_two, rows_three]

        feed = lax.all_gather(near, "dp", axis=0, tiled=True)
        bias_wide = expand_bias.astype(WIDE)

        bias_full = jnp.concatenate([bias_qv[0], jnp.zeros_like(bias_qv[0]), bias_qv[1]])
        starts = ((jnp.arange(n_t) ^ place) * rows).astype(jnp.int32)
        head_ids = (place * heads + jnp.arange(heads) + 1).astype(WIDE)
        slopes = jnp.exp2(-8.0 * head_ids / HEADS)
        normed_all, mixed, context, totals, *branch_low = call_kernel(
            functools.partial(attend_kernel, heads),
            [slopes, starts],
            [rows_list[0], gain_one[None], shift_one[None], full, bias_full[None]]
            + rows_list[1:],
            [
                shape(tokens, width, kind=LOW),
                shape(tokens, 3 * local, kind=LOW),
                shape(tokens, local, kind=LOW),
                shape(heads, tokens),
            ]
            + parts(),
            [pltpu.VMEM((local, tokens), LOW)],
            2 * tokens * width * 4 * local + 4 * tokens * tokens * local,
        )
        tops_one, tops_two = swap_z(top_low, 1, "tops"), swap_z(top_low, 2, "tops")
        branch_low[3], tops_one, tops_two = together(branch_low[3], tops_one, tops_two)
        both = fold_far(branch_low, "branch")
        one, two = fold_near(branch_low, both, "branch")
        one, two, tops_two, feed = together(one, two, tops_two, feed)
        tops_far = swap_z(tops_two, 1, "tops_far")
        tops_list = [top_low, tops_one, tops_two, tops_far]
        branch = fold_end(branch_low, one, two)
        middle = block_input.astype(WIDE) + branch + project_out_bias.astype(WIDE)

        unit_two, scale_two = stats(middle)
        second_low = (unit_two * gain_two + shift_two).astype(LOW)
        second_list = gather_z(second_low, "second")
        active, hidden_grad, *second_parts, expand_bias_part = call_kernel(
            feed_kernel,
            [],
            [second_list[0], feed, bias_wide[None], tops_list[0]]
            + [block for two in zip(second_list[1:], tops_list[1:]) for block in two],
            [shape(tokens, wide, kind=LOW), shape(tokens, wide, kind=LOW)]
            + parts()
            + [shape(1, wide)],
            [],
            6 * tokens * width * wide,
        )
        second_low_parts = second_parts
        both = fold_far(second_low_parts, "second_grad")
        both, hidden_grad, active = together(both, hidden_grad, active)
        one, two = fold_near(second_low_parts, both, "second_grad")
        feed_grad = weight_grads(second_list, hidden_grad, tops_list, active)
        one, two, *feed_grad = together(one, two, *feed_grad)
        second_grad = fold_end(second_low_parts, one, two)
        feed_grad = jnp.concatenate(feed_grad, axis=1)
        feed_sum = lax.psum_scatter(feed_grad, "dp", scatter_dimension=0, tiled=True)
        feed_sum = feed_sum.astype(WIDE)

        upstream = output_cotangent.astype(WIDE)
        middle_grad = upstream + norm_back(second_grad, gain_two, unit_two, scale_two)
        middle_list = gather_z(middle_grad.astype(LOW), "middle")
        middle_list[1], middle_list[2], active = together(middle_list[1], middle_list[2], active)
        middle_list[3] = swap_z(middle_list[2], 1, "middle_far")
        shrunk = jnp.einsum("sf,df->sd", active, feed[:, wide:], preferred_element_type=WIDE)
        shrunk = shrunk.reshape(n_t, rows, width)
        shrunk = [shrunk[0]] + [shrunk[k].astype(LOW) for k in range(1, n_t)]
        middle_list[3], *shrunk[1:] = together(middle_list[3], *shrunk[1:])
        shrunk_both = fold_far(shrunk, "shrunk")

        mixed_grad, *first_low, mixed_sums, gain_parts = call_kernel(
            functools.partial(attend_back_kernel, heads),
            [slopes, starts],
            [middle_list[0], full] + middle_list[1:] + [mixed, totals] + rows_list,
            [shape(tokens, 3 * local, kind=LOW)]
            + parts()
            + [shape(1, 3 * local), shape(2, width)],
            [pltpu.VMEM((tokens, local), LOW), pltpu.VMEM((local, tokens), LOW)],
            2 * tokens * width * 4 * local + 10 * tokens * tokens * local,
            58,
        )
        mixed_sums = mixed_sums[0]
        slot = jnp.arange(n_t)[:, None]
        bias_slots = jnp.where(slot == place, expand_bias_part, 0.0)
        qv_parts = jnp.stack([mixed_sums[:local], mixed_sums[2 * local :]])
        qv_slots = jnp.where(slot[None] == place, qv_parts[:, None], 0.0)
        early = [
            jnp.sum(middle_grad, axis=0),
            jnp.sum(second_grad * unit_two, axis=0),
            jnp.sum(second_grad, axis=0),
            jnp.sum(upstream, axis=0),
        ]
        vectors = jnp.concatenate(
            [gain_parts, jnp.stack(early), bias_slots.reshape(-1, width), qv_slots.reshape(2, -1)],
            axis=0,
        )
        first_low[3], shrunk_both, shrunk[1], mixed_grad, vectors = together(
            first_low[3], shrunk_both, shrunk[1], mixed_grad, vectors
        )
        both = fold_far(first_low, "first_grad")
        shrunk_one, shrunk_two = fold_near(shrunk, shrunk_both, "shrunk")
        vectors = vectors + swap_z(vectors, 1, "vectors")
        in_grad, out_grad = weight_grads([normed_all], mixed_grad, middle_list, context)
        blocks = n_dp // 2
        grads = jnp.concatenate([in_grad, out_grad], axis=1).reshape(blocks, 2, -1, 4 * local)
        mine = lax.dynamic_slice_in_dim(grads, core, 1, 1)
        other = lax.dynamic_slice_in_dim(grads, 1 - core, 1, 1)
        both, other, vectors, shrunk_one, shrunk_two = together(
            both, other, vectors, shrunk_one, shrunk_two
        )
        first_one, first_two = fold_near(first_low, both, "first_grad")
        swapped = swap_dp(other, 1, "att_grad")
        vectors = vectors + swap_dp(vectors, 1, "vectors")
        grads = (mine.astype(WIDE) + swapped.astype(WIDE)).astype(LOW)
        grads = grads.reshape(blocks, -1, 4 * local)
        attend = Fold(grads[:, :, : 2 * local], grads[:, :, 2 * local :], "att_grad")
        (vectors,) = gate(attend, vectors)
        attend.go()
        for mask in bits[:1]:
            vectors = vectors + swap_dp(vectors, mask, "vectors")
        attend.land()
        first_one, first_two, vectors = gate(attend, first_one, first_two, vectors)
        for mask in bits[1:]:
            vectors = vectors + swap_dp(vectors, mask, "vectors")
        vectors = vectors + swap_z(vectors, 2, "vectors")
        sum_a, sum_b = attend.finish()
        in_sum = jnp.concatenate([sum_a, sum_b[:, :local]], axis=1).astype(WIDE)
        out_sum = sum_b[:, local:].astype(WIDE).T
        result = middle + fold_end(shrunk, shrunk_one, shrunk_two) + shrink_bias.astype(WIDE)
        result = result.astype(LOW)
        first_grad = fold_end(first_low, first_one, first_two)

        unit, scale = stats(block_input.astype(WIDE))
        input_grad = middle_grad + norm_back(first_grad, gain_one, unit, scale)
        bias_slots = vectors[6:-2].reshape(n_t, wide)
        expand_bias_sum = lax.dynamic_index_in_dim(bias_slots, place, 0, keepdims=False)
        qv_slots = vectors[-2:].reshape(2, n_t, local)
        qv_sum = lax.dynamic_index_in_dim(qv_slots, place, 1, keepdims=False)
        return (
            result,
            input_grad.astype(LOW),
            vectors[0],
            vectors[1],
            in_sum.reshape(project_in.shape),
            qv_sum,
            out_sum,
            vectors[2],
            vectors[3],
            vectors[4],
            feed_sum[:, :wide],
            expand_bias_sum,
            feed_sum[:, wide:].T,
            vectors[5],
        )

    return body


def solution(mesh):
    placed = (
        P(("dp", "tensor"), None),
        P(("dp", "tensor"), None),
        P(),
        P(),
        P("dp", None, "tensor"),
        P(None, "tensor"),
        P("tensor", "dp"),
        P(),
        P(),
        P(),
        P("dp", "tensor"),
        P("tensor"),
        P("tensor", "dp"),
        P(),
    )
    return jax.shard_map(
        make_body(mesh.shape["dp"], mesh.shape["tensor"]),
        mesh=mesh,
        in_specs=placed,
        out_specs=(
            P(("dp", "tensor"), None),
            P(("dp", "tensor"), None),
            P(),
            P(),
            P("dp", None, "tensor"),
            P(None, "tensor"),
            P("tensor", "dp"),
            P(),
            P(),
            P(),
            P("dp", "tensor"),
            P("tensor"),
            P("tensor", "dp"),
            P(),
        ),
        check_vma=False,
    )
```

```python
import functools
import math

import jax
import jax.numpy as jnp
from jax import lax
from jax.experimental import pallas as pl
from jax.experimental.pallas import tpu as pltpu
from jax.sharding import PartitionSpec as P

HEADS = 16
HEAD = 64
AXES = ("dp", "tensor")
LOW = jnp.bfloat16
WIDE = jnp.float32


def together(*values):
    return lax.optimization_barrier(values)


def stats(rows):
    average = jnp.mean(rows, axis=-1, keepdims=True)
    centered = rows - average
    variance = jnp.mean(centered * centered, axis=-1, keepdims=True)
    scale = lax.rsqrt(variance + 1e-05)
    return centered * scale, scale


def norm_back(grad, gain, unit, scale):
    inner = grad * gain
    first = jnp.mean(inner, axis=-1, keepdims=True)
    second = jnp.mean(inner * unit, axis=-1, keepdims=True)
    return scale * (inner - first - unit * second)


def gelu_local(hidden):
    return jax.nn.gelu(hidden, approximate=True)


def clean_dot(x, y, contract):
    return lax.dot_general(x, y, (contract, ((), ())), preferred_element_type=WIDE)


def row_norm(rows):
    centered = rows - jnp.mean(rows, axis=-1, keepdims=True)
    variance = jnp.mean(centered * centered, axis=-1, keepdims=True)
    return centered * lax.rsqrt(variance + 1e-05)


def distances(starts, rows):
    count = starts.shape[0]
    down = lax.broadcasted_iota(jnp.int32, (rows, 1), 0)
    across = lax.broadcasted_iota(jnp.int32, (1, rows), 1)
    down = jnp.concatenate([down + starts[k] for k in range(count)], axis=0)
    across = jnp.concatenate([across + starts[k] for k in range(count)], axis=1)
    return (across - down).astype(WIDE)


def attend_kernel(
    heads, slopes, starts, row_a, gain, shift, weights, bias, row_b, row_c, row_d,
    normed, mixed, context, totals, branch_a, branch_b, branch_c, branch_d, turned,
):
    rows = row_a.shape[0]
    local = heads * HEAD
    for k, block in enumerate((row_a, row_b, row_c, row_d)):
        unit = row_norm(block[...].astype(WIDE))
        low = (unit * gain[...] + shift[...]).astype(LOW)
        here = pl.ds(k * rows, rows)
        normed[here, :] = low
        out = jnp.dot(low, weights[:, : 3 * local], preferred_element_type=WIDE)
        mixed[here, :] = (out + bias[...]).astype(LOW)
    distance = distances(starts, rows)
    allowed = distance >= 0
    for h in range(heads):
        query = mixed[:, pl.ds(h * HEAD, HEAD)]
        key = mixed[:, pl.ds(local + h * HEAD, HEAD)]
        value = mixed[:, pl.ds(2 * local + h * HEAD, HEAD)]
        scores = clean_dot(key, query, ((1,), (1,))) * HEAD ** (-0.5) - slopes[h] * distance
        scores = jnp.where(allowed, scores, -1e30)
        top = jnp.max(scores, axis=0, keepdims=True)
        grown = jnp.exp(scores - top)
        total = jnp.sum(grown, axis=0, keepdims=True)
        totals[h : h + 1, :] = top + jnp.log(total)
        soft = (grown * (1.0 / total)).astype(LOW)
        turned[h * HEAD : (h + 1) * HEAD, :] = jnp.dot(
            value.T, soft, preferred_element_type=WIDE
        ).astype(LOW)
    context[...] = turned[...].T
    for k, block in enumerate((branch_a, branch_b, branch_c, branch_d)):
        out = clean_dot(context[pl.ds(k * rows, rows), :], weights[:, 3 * local :], ((1,), (1,)))
        block[...] = out.astype(block.dtype)


def attend_back_kernel(
    heads, slopes, starts, grad_a, weights, grad_b, grad_c, grad_d, mixed, totals,
    row_a, row_b, row_c, row_d,
    mixed_grad, first_a, first_b, first_c, first_d, sums, vectors, back, turned,
):
    rows = row_a.shape[0]
    local = heads * HEAD
    for k, block in enumerate((grad_a, grad_b, grad_c, grad_d)):
        out = jnp.dot(block[...], weights[:, 3 * local :], preferred_element_type=WIDE)
        back[pl.ds(k * rows, rows), :] = out.astype(LOW)
    distance = distances(starts, rows)
    allowed = distance >= 0
    for h in range(heads):
        query = mixed[:, pl.ds(h * HEAD, HEAD)]
        key = mixed[:, pl.ds(local + h * HEAD, HEAD)]
        value = mixed[:, pl.ds(2 * local + h * HEAD, HEAD)]
        given = back[:, pl.ds(h * HEAD, HEAD)]
        scores = clean_dot(key, query, ((1,), (1,))) * HEAD ** (-0.5) - slopes[h] * distance
        scores = jnp.where(allowed, scores, -1e30)
        soft = jnp.exp(scores - totals[h : h + 1, :])
        value_grad = jnp.dot(soft.astype(LOW), given, preferred_element_type=WIDE)
        soft_grad = clean_dot(value, given, ((1,), (1,)))
        middle = jnp.sum(soft * soft_grad, axis=0, keepdims=True)
        score_grad = (soft * (soft_grad - middle)).astype(LOW)
        key_grad = jnp.dot(score_grad, query, preferred_element_type=WIDE) * HEAD ** (-0.5)
        query_grad = jnp.dot(key.T, score_grad, preferred_element_type=WIDE) * HEAD ** (-0.5)
        turned[h * HEAD : (h + 1) * HEAD, :] = query_grad.astype(LOW)
        mixed_grad[:, pl.ds(local + h * HEAD, HEAD)] = key_grad.astype(LOW)
        mixed_grad[:, pl.ds(2 * local + h * HEAD, HEAD)] = value_grad.astype(LOW)
    mixed_grad[:, :local] = turned[...].T
    sums[...] = jnp.sum(mixed_grad[...].astype(WIDE), axis=0, keepdims=True)
    gain_sum = jnp.zeros(vectors.shape[1:], WIDE)[None]
    shift_sum = gain_sum
    for k, (block, unit) in enumerate(
        ((first_a, row_a), (first_b, row_b), (first_c, row_c), (first_d, row_d))
    ):
        here = mixed_grad[pl.ds(k * rows, rows), :]
        out = clean_dot(here, weights[:, : 3 * local], ((1,), (1,)))
        block[...] = out.astype(block.dtype)
        unit = row_norm(unit[...].astype(WIDE))
        gain_sum = gain_sum + jnp.sum(out * unit, axis=0, keepdims=True)
        shift_sum = shift_sum + jnp.sum(out, axis=0, keepdims=True)
    vectors[0:1, :] = gain_sum
    vectors[1:2, :] = shift_sum


def feed_kernel(count, row, weights, bias, top, *refs):
    blocks = [(row, top)] + [(refs[2 * k], refs[2 * k + 1]) for k in range(count - 1)]
    active, back, *parts, sums = refs[2 * count - 2 :]
    rows = row.shape[0]
    wide = active.shape[1]
    total = jnp.zeros((1, wide), WIDE)
    for k, ((row, top), part) in enumerate(zip(blocks, parts)):
        here = pl.ds(k * rows, rows)
        hidden = jnp.dot(row[...], weights[:, :wide], preferred_element_type=WIDE) + bias[...]
        square = hidden * hidden
        curve = jnp.tanh(0.7978845608028654 * hidden * (1.0 + 0.044715 * square))
        half = 0.5 * (1.0 + curve)
        active[here, :] = (hidden * half).astype(LOW)
        slope = 0.7978845608028654 * (1.0 + 3 * 0.044715 * square)
        slope = half + 0.5 * hidden * (1.0 - curve * curve) * slope
        grad = jnp.dot(top[...], weights[:, wide:], preferred_element_type=WIDE)
        grad = (grad * slope).astype(LOW)
        back[here, :] = grad
        total = total + jnp.sum(grad.astype(WIDE), axis=0, keepdims=True)
        out = clean_dot(grad, weights[:, :wide], ((1,), (1,)))
        part[...] = out.astype(part.dtype)
    sums[...] = total


class Late:
    def __init__(self, copy, ref):
        self.copy, self.ref, self.shape = copy, ref, ref.shape

    def here(self):
        if self.copy is not None:
            self.copy.wait()
            self.copy = None
        return self.ref

    def __getitem__(self, index):
        return self.here()[index]


def call_kernel(body, scalars, arrays, outs, scratch, flops, mega=32):
    count, first = len(arrays), len(scalars)

    def kernel(*refs):
        sources = refs[first : first + count]
        results = refs[first + count : first + count + len(outs)]
        rest = refs[first + count + len(outs) :]
        held, arrived, own = rest[:count], rest[count], rest[count + 1 :]
        inputs = []
        for k in range(count):
            copy = pltpu.make_async_copy(sources[k], held[k], arrived.at[k])
            copy.start()
            inputs.append(Late(copy, held[k]))
        body(*refs[:first], *inputs, *results, *own)
        for late in inputs:
            late.here()

    def space(array):
        return pl.BlockSpec(array.shape, lambda _: (0,) * len(array.shape))

    sizes = sum(math.prod(a.shape) * a.dtype.itemsize for a in list(arrays) + list(outs))
    return pl.pallas_call(
        kernel,
        grid=(1,),
        in_specs=[pl.BlockSpec(memory_space=pltpu.SMEM)] * first
        + [pl.BlockSpec(memory_space=pltpu.HBM)] * count,
        out_specs=[space(array) for array in outs],
        out_shape=outs,
        scratch_shapes=[pltpu.VMEM(array.shape, array.dtype) for array in arrays]
        + [pltpu.SemaphoreType.DMA((count,))]
        + scratch,
        compiler_params=pltpu.CompilerParams(vmem_limit_bytes=mega << 20),
        cost_estimate=pl.CostEstimate(flops=flops, bytes_accessed=sizes, transcendentals=0),
    )(*scalars, *arrays)


def grads_kernel(steps, counts, *refs):
    refs = list(refs)
    blocks, ys, others, vs = [[refs.pop(0) for _ in range(count)] for count in counts]
    out_ref, more_ref, turned = refs
    step = pl.program_id(0)

    def turn(pieces):
        first = 0
        for piece in pieces:
            size = piece.shape[0]
            turned[:, first : first + size] = piece[...].T
            first += size

    def product(pieces):
        total, first = 0.0, 0
        for piece in pieces:
            size = piece.shape[0]
            total = total + jnp.dot(
                turned[:, first : first + size], piece[...], preferred_element_type=WIDE
            )
            first += size
        return total.astype(LOW)

    @pl.when(step == 0)
    def _():
        turn(blocks)

    @pl.when(step == steps)
    def _():
        turn(others)

    @pl.when(step < steps)
    def _():
        out_ref[...] = product(ys)

    @pl.when(step >= steps)
    def _():
        more_ref[...] = product(vs)


def weight_grads(blocks, ys, others, vs):
    tokens, width = sum(block.shape[0] for block in blocks), blocks[0].shape[1]
    columns = 256
    steps, more = ys[0].shape[1] // columns, vs[0].shape[1] // columns

    def whole(block):
        return pl.BlockSpec(block.shape, lambda j: (0, 0))

    def early(block):
        return pl.BlockSpec((block.shape[0], columns), lambda j: (0, jnp.minimum(j, steps - 1)))

    def late(block):
        return pl.BlockSpec((block.shape[0], columns), lambda j: (0, jnp.maximum(j - steps, 0)))

    groups = ((blocks, whole), (ys, early), (others, whole), (vs, late))
    return pl.pallas_call(
        functools.partial(grads_kernel, steps, [len(group) for group, _ in groups]),
        grid=(steps + more,),
        in_specs=[spec(block) for group, spec in groups for block in group],
        out_specs=[
            pl.BlockSpec((width, columns), lambda j: (0, jnp.minimum(j, steps - 1))),
            pl.BlockSpec((width, columns), lambda j: (0, jnp.maximum(j - steps, 0))),
        ],
        out_shape=[jax.ShapeDtypeStruct((width, z[0].shape[1]), LOW) for z in (ys, vs)],
        scratch_shapes=[pltpu.VMEM((width, tokens), LOW)],
        compiler_params=pltpu.CompilerParams(vmem_limit_bytes=24 << 20),
        cost_estimate=pl.CostEstimate(
            flops=2 * tokens * width * columns * (steps + more),
            bytes_accessed=2 * width * (2 * tokens + columns * (steps + more)),
            transcendentals=0,
        ),
    )(*blocks, *ys, *others, *vs)


def make_body(n_dp, n_t):
    bits = [1 << k for k in range(1, n_dp.bit_length() - 1)]

    def send(value, target, name):
        pairs = []
        for d in range(n_dp):
            for t in range(n_t):
                goal = target(d, t)
                if goal is not None:
                    pairs.append((d * n_t + t, goal[0] * n_t + goal[1]))
        with jax.named_scope(name):
            return lax.ppermute(value, AXES, pairs)

    def swap_z(value, mask, name):
        return send(value, lambda d, t: (d, t ^ mask), f"{name}_z{mask}")

    def swap_dp(value, mask, name):
        return send(value, lambda d, t: (d ^ mask, t), f"{name}_d{mask}")

    def bit_of(mask):
        return (lax.axis_index("dp") & mask) != 0

    class Spread:
        def __init__(self, first, second, name):
            lead = (1,) * len(bits)
            self.ops = [first.reshape(lead + first.shape), second.reshape(lead + second.shape)]
            self.shapes = (first.shape, second.shape)
            self.name = name
            self.left = list(zip(bits[::-1], bits))

        def go(self):
            self.masks = self.left.pop(0)
            self.others = [
                swap_dp(value, mask, self.name + label)
                for value, mask, label in zip(self.ops, self.masks, ("_a", "_b"))
            ]

        def land(self):
            for k, (mask, other) in enumerate(zip(self.masks, self.others)):
                axis = len(bits) - 1 - bits.index(mask)
                own, flag = self.ops[k], bit_of(mask)
                self.ops[k] = jnp.concatenate(
                    [jnp.where(flag, other, own), jnp.where(flag, own, other)], axis=axis
                )

        def finish(self):
            while self.left:
                self.go()
                self.land()
                self.ops = list(together(*self.ops))
            return [
                value.reshape((-1,) + shape[1:]) for value, shape in zip(self.ops, self.shapes)
            ]

    class Fold:
        def __init__(self, first, second, name):
            lead = (2,) * len(bits)
            self.shapes = (first.shape, second.shape)
            self.values = [
                first.reshape(lead + first.shape[1:]),
                second.reshape(lead + second.shape[1:]),
            ]
            self.name = name
            self.left = list(zip(bits, bits[::-1]))
            self.cut()

        def cut(self):
            self.ops, self.keep = [], []
            for value, mask in zip(self.values, self.left[0]):
                axis = len(bits) - 1 - bits.index(mask)
                place = (lax.axis_index("dp") // mask) % 2
                self.keep.append(lax.dynamic_slice_in_dim(value, place, 1, axis))
                self.ops.append(lax.dynamic_slice_in_dim(value, 1 - place, 1, axis).astype(LOW))

        def go(self):
            masks = self.left.pop(0)
            self.others = [
                swap_dp(value, mask, self.name + label)
                for value, mask, label in zip(self.ops, masks, ("_a", "_b"))
            ]

        def land(self):
            self.values = [
                (keep.astype(WIDE) + other.astype(WIDE)).astype(LOW)
                for keep, other in zip(self.keep, self.others)
            ]
            self.ops = list(self.values)
            if self.left:
                self.cut()

        def finish(self):
            while self.left:
                self.go()
                self.land()
                self.ops = list(together(*self.ops))
            return [value.reshape(shape[1:]) for value, shape in zip(self.ops, self.shapes)]

    def gate(chain, *values):
        count = len(chain.ops)
        *ops, = together(*chain.ops, *values)
        chain.ops = ops[:count]
        return ops[count:]

    def gather_z(value, name):
        one = swap_z(value, 1, name)
        two = swap_z(value, 2, name)
        return [value, one, two, swap_z(two, 1, name + "_far")]

    def fold_far(parts, name):
        far = swap_z(parts[3].astype(LOW), 1, name + "_far")
        return (parts[2].astype(WIDE) + far.astype(WIDE)).astype(LOW)

    def fold_near(parts, both, name):
        two = swap_z(both, 2, name)
        one = swap_z(parts[1].astype(LOW), 1, name)
        return one, two

    def fold_end(parts, one, two):
        return parts[0].astype(WIDE) + one.astype(WIDE) + two.astype(WIDE)

    def body(
        block_input,
        output_cotangent,
        first_gain,
        first_shift,
        project_in,
        query_value_bias,
        project_out,
        project_out_bias,
        second_gain,
        second_shift,
        expand_weight,
        expand_bias,
        shrink_weight,
        shrink_bias,
    ):
        rows, width = block_input.shape
        local = project_out.shape[0]
        wide = expand_weight.shape[1]
        heads = local // HEAD
        core = lax.axis_index("dp") % 2
        place = lax.axis_index("tensor")
        gain_one, shift_one = first_gain.astype(WIDE), first_shift.astype(WIDE)
        gain_two, shift_two = second_gain.astype(WIDE), second_shift.astype(WIDE)
        bias_qv = query_value_bias.astype(WIDE)
        tokens = n_t * rows

        def shape(*dims, kind=WIDE):
            return jax.ShapeDtypeStruct(dims, kind)

        def parts():
            return [shape(rows, width)] + [shape(rows, width, kind=LOW)] * (n_t - 1)


        part_in = project_in.reshape(project_in.shape[0], 3 * local)
        part_a = part_in[:, : 2 * local]
        part_b = jnp.concatenate([part_in[:, 2 * local :], project_out.T], axis=1)
        near = jnp.concatenate([expand_weight, shrink_weight.T], axis=1)
        rows_one = swap_z(block_input, 1, "rows")
        rows_two = swap_z(block_input, 2, "rows")
        attend = Spread(part_a[None], part_b[None], "att")
        attend.go()
        attend.land()
        rows_one, rows_two, near = gate(attend, rows_one, rows_two, near)
        rows_three = swap_z(rows_two, 1, "rows_far")
        full_a, full_b = attend.finish()
        full_a, full_b, near, rows_three, top_low = together(
            full_a, full_b, near, rows_three, output_cotangent
        )
        pair = jnp.concatenate([full_a, full_b], axis=-1)
        mate = swap_dp(pair, 1, "att")
        full = jnp.stack([jnp.where(core == 0, pair, mate), jnp.where(core == 0, mate, pair)], 1)
        full = full.reshape(width, 4 * local)
        rows_list = [block_input, rows_one, rows_two, rows_three]

        feed = lax.all_gather(near, "dp", axis=0, tiled=True)
        bias_wide = expand_bias.astype(WIDE)

        bias_full = jnp.concatenate([bias_qv[0], jnp.zeros_like(bias_qv[0]), bias_qv[1]])
        starts = ((jnp.arange(n_t) ^ place) * rows).astype(jnp.int32)
        head_ids = (place * heads + jnp.arange(heads) + 1).astype(WIDE)
        slopes = jnp.exp2(-8.0 * head_ids / HEADS)
        normed_all, mixed, context, totals, *branch_low = call_kernel(
            functools.partial(attend_kernel, heads),
            [slopes, starts],
            [rows_list[0], gain_one[None], shift_one[None], full, bias_full[None]]
            + rows_list[1:],
            [
                shape(tokens, width, kind=LOW),
                shape(tokens, 3 * local, kind=LOW),
                shape(tokens, local, kind=LOW),
                shape(heads, tokens),
            ]
            + parts(),
            [pltpu.VMEM((local, tokens), LOW)],
            2 * tokens * width * 4 * local + 4 * tokens * tokens * local,
        )
        tops_one, tops_two = swap_z(top_low, 1, "tops"), swap_z(top_low, 2, "tops")
        branch_low[3], tops_one, tops_two = together(branch_low[3], tops_one, tops_two)
        both = fold_far(branch_low, "branch")
        one, two = fold_near(branch_low, both, "branch")
        one, two, tops_two, feed = together(one, two, tops_two, feed)
        tops_far = swap_z(tops_two, 1, "tops_far")
        tops_list = [top_low, tops_one, tops_two, tops_far]
        branch = fold_end(branch_low, one, two)
        middle = block_input.astype(WIDE) + branch + project_out_bias.astype(WIDE)

        unit_two, scale_two = stats(middle)
        second_low = (unit_two * gain_two + shift_two).astype(LOW)
        second_list = gather_z(second_low, "second")
        def feed_forward(row_blocks, top_blocks, outs):
            count = len(row_blocks)
            pairs = list(zip(row_blocks, top_blocks))
            return call_kernel(
                functools.partial(feed_kernel, count),
                [],
                [pairs[0][0], feed, bias_wide[None], pairs[0][1]]
                + [block for pair in pairs[1:] for block in pair],
                [shape(count * rows, wide, kind=LOW)] * 2 + outs + [shape(1, wide)],
                [],
                6 * count * rows * width * wide,
            )

        active, hidden_grad, *second_parts, sums = feed_forward(
            second_list[:3], tops_list[:3], parts()[:3]
        )
        active_far, hidden_far, part_far, sums_far = feed_forward(
            second_list[3:], tops_list[3:], parts()[3:]
        )
        second_parts.append(part_far)
        expand_bias_part = sums + sums_far
        second_low_parts = second_parts
        both = fold_far(second_low_parts, "second_grad")
        both, hidden_grad, active, hidden_far, active_far = together(
            both, hidden_grad, active, hidden_far, active_far
        )
        one, two = fold_near(second_low_parts, both, "second_grad")
        feed_grad = weight_grads(
            second_list, [hidden_grad, hidden_far], tops_list, [active, active_far]
        )
        one, two, *feed_grad = together(one, two, *feed_grad)
        second_grad = fold_end(second_low_parts, one, two)
        feed_grad = jnp.concatenate(feed_grad, axis=1)
        feed_sum = lax.psum_scatter(feed_grad, "dp", scatter_dimension=0, tiled=True)
        feed_sum = feed_sum.astype(WIDE)

        upstream = output_cotangent.astype(WIDE)
        middle_grad = upstream + norm_back(second_grad, gain_two, unit_two, scale_two)
        middle_list = gather_z(middle_grad.astype(LOW), "middle")
        middle_list[1], middle_list[2], active, active_far = together(
            middle_list[1], middle_list[2], active, active_far
        )
        middle_list[3] = swap_z(middle_list[2], 1, "middle_far")
        shrunk = jnp.einsum("sf,df->sd", active, feed[:, wide:], preferred_element_type=WIDE)
        shrunk = shrunk.reshape(n_t - 1, rows, width)
        shrunk_last = jnp.einsum(
            "sf,df->sd", active_far, feed[:, wide:], preferred_element_type=WIDE
        )
        shrunk = [shrunk[0], shrunk[1].astype(LOW), shrunk[2].astype(LOW), shrunk_last.astype(LOW)]
        middle_list[3], *shrunk[1:] = together(middle_list[3], *shrunk[1:])
        shrunk_both = fold_far(shrunk, "shrunk")

        mixed_grad, *first_low, mixed_sums, gain_parts = call_kernel(
            functools.partial(attend_back_kernel, heads),
            [slopes, starts],
            [middle_list[0], full] + middle_list[1:] + [mixed, totals] + rows_list,
            [shape(tokens, 3 * local, kind=LOW)]
            + parts()
            + [shape(1, 3 * local), shape(2, width)],
            [pltpu.VMEM((tokens, local), LOW), pltpu.VMEM((local, tokens), LOW)],
            2 * tokens * width * 4 * local + 10 * tokens * tokens * local,
            58,
        )
        mixed_sums = mixed_sums[0]
        slot = jnp.arange(n_t)[:, None]
        bias_slots = jnp.where(slot == place, expand_bias_part, 0.0)
        qv_parts = jnp.stack([mixed_sums[:local], mixed_sums[2 * local :]])
        qv_slots = jnp.where(slot[None] == place, qv_parts[:, None], 0.0)
        early = [
            jnp.sum(middle_grad, axis=0),
            jnp.sum(second_grad * unit_two, axis=0),
            jnp.sum(second_grad, axis=0),
            jnp.sum(upstream, axis=0),
        ]
        vectors = jnp.concatenate(
            [gain_parts, jnp.stack(early), bias_slots.reshape(-1, width), qv_slots.reshape(2, -1)],
            axis=0,
        )
        first_low[3], shrunk_both, shrunk[1], mixed_grad, vectors = together(
            first_low[3], shrunk_both, shrunk[1], mixed_grad, vectors
        )
        both = fold_far(first_low, "first_grad")
        shrunk_one, shrunk_two = fold_near(shrunk, shrunk_both, "shrunk")
        vectors = vectors + swap_z(vectors, 1, "vectors")
        in_grad, out_grad = weight_grads([normed_all], [mixed_grad], middle_list, [context])
        blocks = n_dp // 2
        grads = jnp.concatenate([in_grad, out_grad], axis=1).reshape(blocks, 2, -1, 4 * local)
        mine = lax.dynamic_slice_in_dim(grads, core, 1, 1)
        other = lax.dynamic_slice_in_dim(grads, 1 - core, 1, 1)
        both, other, vectors, shrunk_one, shrunk_two = together(
            both, other, vectors, shrunk_one, shrunk_two
        )
        first_one, first_two = fold_near(first_low, both, "first_grad")
        swapped = swap_dp(other, 1, "att_grad")
        vectors = vectors + swap_dp(vectors, 1, "vectors")
        grads = (mine.astype(WIDE) + swapped.astype(WIDE)).astype(LOW)
        grads = grads.reshape(blocks, -1, 4 * local)
        attend = Fold(grads[:, :, : 2 * local], grads[:, :, 2 * local :], "att_grad")
        (vectors,) = gate(attend, vectors)
        attend.go()
        for mask in bits[:1]:
            vectors = vectors + swap_dp(vectors, mask, "vectors")
        attend.land()
        first_one, first_two, vectors, feed_sum = gate(
            attend, first_one, first_two, vectors, feed_sum
        )
        for mask in bits[1:]:
            vectors = vectors + swap_dp(vectors, mask, "vectors")
        vectors = vectors + swap_z(vectors, 2, "vectors")
        sum_a, sum_b = attend.finish()
        in_sum = jnp.concatenate([sum_a, sum_b[:, :local]], axis=1).astype(WIDE)
        out_sum = sum_b[:, local:].astype(WIDE).T
        result = middle + fold_end(shrunk, shrunk_one, shrunk_two) + shrink_bias.astype(WIDE)
        result = result.astype(LOW)
        first_grad = fold_end(first_low, first_one, first_two)

        unit, scale = stats(block_input.astype(WIDE))
        input_grad = middle_grad + norm_back(first_grad, gain_one, unit, scale)
        bias_slots = vectors[6:-2].reshape(n_t, wide)
        expand_bias_sum = lax.dynamic_index_in_dim(bias_slots, place, 0, keepdims=False)
        qv_slots = vectors[-2:].reshape(2, n_t, local)
        qv_sum = lax.dynamic_index_in_dim(qv_slots, place, 1, keepdims=False)
        return (
            result,
            input_grad.astype(LOW),
            vectors[0],
            vectors[1],
            in_sum.reshape(project_in.shape),
            qv_sum,
            out_sum,
            vectors[2],
            vectors[3],
            vectors[4],
            feed_sum[:, :wide],
            expand_bias_sum,
            feed_sum[:, wide:].T,
            vectors[5],
        )

    return body


def solution(mesh):
    placed = (
        P(("dp", "tensor"), None),
        P(("dp", "tensor"), None),
        P(),
        P(),
        P("dp", None, "tensor"),
        P(None, "tensor"),
        P("tensor", "dp"),
        P(),
        P(),
        P(),
        P("dp", "tensor"),
        P("tensor"),
        P("tensor", "dp"),
        P(),
    )
    return jax.shard_map(
        make_body(mesh.shape["dp"], mesh.shape["tensor"]),
        mesh=mesh,
        in_specs=placed,
        out_specs=(
            P(("dp", "tensor"), None),
            P(("dp", "tensor"), None),
            P(),
            P(),
            P("dp", None, "tensor"),
            P(None, "tensor"),
            P("tensor", "dp"),
            P(),
            P(),
            P(),
            P("dp", "tensor"),
            P("tensor"),
            P("tensor", "dp"),
            P(),
        ),
        check_vma=False,
    )
```
